512 devices in a mesh: beam: 32 (over x, z_lo), tile: 16 (over z_hi, y, core).
Axes of the slice: x: 4, y: 4, z: 16 (z_hi: 2, z_lo: 8; z = z_hi * 8 + z_lo), core: 2. Of those that a mesh axis runs over, the one named last changes fastest.
Arguments:
- atom_counts: bfloat16 [2, 512, 4096], P(None, 'tile'), may hold values from 0 to 4
- beam_index: int32 [32, 2], P('beam'), may hold values from -16 to 16
- beam_weight: float32 [32], P('beam'), may hold values from 0.3 to 3
- probe_rows: int32 [1024], P('tile'), may hold values from 0 to 16
- probe_cols: int32 [1024], P('tile'), may hold values from 0 to 4095
Outputs:
- intensity: float32 [1024, 256], P('tile', 'beam')
The draws below stay inside these ranges and needn't reach their ends.
All inputs are finite; a program needn't handle non-finite values.
Results may differ from the reference program's by a relative error of at most 0.0003.
Values may be sent and summed in bfloat16 or wider, within the bound.
A program may use at most 64 MiB of HBM per device.

```python
import math
import jax
import jax.numpy as jnp
from jax import lax

BEAM_DEV = 1
ROWS_DEV = 32
NY = 4096
PROBE_DEV = 64
SLICES = 2
CROP = 16
BEAMS = 32
NX = 512
PROBES = 1024


def plant(values, own_key, least, largest):
    longest = values.shape.index(max(values.shape))
    spots = []
    for shift in (0, 1):
        where = [jax.random.randint(jax.random.fold_in(own_key, axis), (), 0, length) for axis, length in enumerate(values.shape)]
        where[longest] = (where[longest] + shift) % values.shape[longest]
        spots.append(tuple(where))
    return values.at[spots[0]].set(least).at[spots[1]].set(largest)


def block_scale(rng, dims, pieces, smallest, top_value):
    gain = 1.0
    for position, shards_of in pieces:
        steps = jax.random.uniform(jax.random.fold_in(jax.random.fold_in(rng, 6), position), (shards_of,), jnp.float32, smallest / len(pieces), top_value / len(pieces))
        gain = gain * jnp.repeat(jnp.exp(steps), dims[position] // shards_of).reshape((-1,) + (1,) * (len(dims) - 1 - position))
    return gain


def setup_inputs(seed: int = 0) -> dict:
    splits = jax.random.split(jax.random.key(seed), 6)
    return {
        "atom_counts": jnp.clip(4.0 * jax.random.uniform(splits[0], (SLICES, NX, NY), jnp.float32) ** block_scale(splits[0], (SLICES, NX, NY), ((1, 16),), -0.2, 0.2), 0.0, 4.0).astype(jnp.bfloat16),
        "beam_index": plant(jax.random.randint(splits[1], (BEAMS, 2), -16, 17), jax.random.fold_in(splits[1], 1), -16, 16).astype(jnp.int32),
        "beam_weight": jnp.clip(jnp.exp(math.log(3.0) - 2.3025851 * jax.random.uniform(splits[2], (BEAMS,), jnp.float32) ** block_scale(splits[2], (BEAMS,), ((0, 32),), -0.2, 0.2)), 0.3, 3.0),
        "probe_rows": plant(jax.random.randint(splits[3], (PROBES,), 0, ROWS_DEV - CROP + 1), jax.random.fold_in(splits[3], 1), 0, ROWS_DEV - CROP).astype(jnp.int32),
        "probe_cols": plant(jax.random.randint(splits[4], (PROBES,), 0, NY), jax.random.fold_in(splits[4], 1), 0, NY - 1).astype(jnp.int32),
    }


def make_taps():
    blur_raw = [math.exp(-(offset_index - 5) ** 2 / 4.5) for offset_index in range(11)]
    blur_total = sum(blur_raw)
    spread_raw = [math.exp(-(offset_index - 5) ** 2 / 18.0) for offset_index in range(11)]
    spread_total = sum(spread_raw)
    blur_list = [entry_value / blur_total for entry_value in blur_raw]
    cos_list = [spread_raw[offset_index] / spread_total * math.cos(0.35 * (offset_index - 5) ** 2) for offset_index in range(11)]
    sin_list = [spread_raw[offset_index] / spread_total * math.sin(0.35 * (offset_index - 5) ** 2) for offset_index in range(11)]
    return blur_list, cos_list, sin_list


def blur_axis(values, axis_number):
    blur_taps, cos_taps, sin_taps = make_taps()
    result = blur_taps[0] * jnp.roll(values, 5, axis=axis_number)
    for offset_index in range(1, 11):
        result = result + blur_taps[offset_index] * jnp.roll(values, 5 - offset_index, axis=axis_number)
    return result


def spread_axis(real_part, imag_part, axis_number):
    blur_taps, cos_taps, sin_taps = make_taps()
    out_real = jnp.zeros_like(real_part)
    out_imag = jnp.zeros_like(imag_part)
    for offset_index in range(11):
        shift_real = jnp.roll(real_part, 5 - offset_index, axis=axis_number)
        shift_imag = jnp.roll(imag_part, 5 - offset_index, axis=axis_number)
        out_real = out_real + cos_taps[offset_index] * shift_real - sin_taps[offset_index] * shift_imag
        out_imag = out_imag + cos_taps[offset_index] * shift_imag + sin_taps[offset_index] * shift_real
    return out_real, out_imag


def reference(atom_counts, beam_index, beam_weight, probe_rows, probe_cols):
    counts_float = atom_counts.astype(jnp.float32)
    blurred = blur_axis(blur_axis(counts_float, 1), 2)
    cos_trans = jnp.cos(0.6 * blurred)
    sin_trans = jnp.sin(0.6 * blurred)
    row_grid = jnp.arange(NX, dtype=jnp.int32)
    col_grid = jnp.arange(NY, dtype=jnp.int32)
    probe_total = probe_rows.shape[0]
    global_rows = (jnp.arange(probe_total, dtype=jnp.int32) // PROBE_DEV) * ROWS_DEV + probe_rows
    crop_rows = global_rows[:, None] + jnp.arange(CROP, dtype=jnp.int32)[None, :]
    crop_cols = (probe_cols[:, None] + jnp.arange(CROP, dtype=jnp.int32)[None, :]) % NY

    def one_block(block):
        indices, weights = block
        row_phase = ((indices[:, 0:1] * row_grid[None, :]) % NX).astype(jnp.float32) / NX
        col_phase = ((indices[:, 1:2] * col_grid[None, :]) % NY).astype(jnp.float32) / NY
        angle_grid = 2.0 * math.pi * (row_phase[:, :, None] + col_phase[:, None, :])
        real_part = jnp.cos(angle_grid)
        imag_part = jnp.sin(angle_grid)
        for slice_index in range(SLICES):
            cos_now = cos_trans[slice_index]
            sin_now = sin_trans[slice_index]
            real_part, imag_part = real_part * cos_now - imag_part * sin_now, real_part * sin_now + imag_part * cos_now
            real_part, imag_part = spread_axis(real_part, imag_part, 1)
            real_part, imag_part = spread_axis(real_part, imag_part, 2)
        crop_real = real_part[:, crop_rows[:, :, None], crop_cols[:, None, :]]
        crop_imag = imag_part[:, crop_rows[:, :, None], crop_cols[:, None, :]]
        probe_phase = 2.0 * math.pi * (((indices[:, 0:1] * global_rows[None, :]) % NX).astype(jnp.float32) / NX + ((indices[:, 1:2] * probe_cols[None, :]) % NY).astype(jnp.float32) / NY)
        coef_real = weights[:, None] * jnp.cos(probe_phase)
        coef_imag = -weights[:, None] * jnp.sin(probe_phase)
        exit_real = jnp.einsum("bp,bpuv->puv", coef_real, crop_real) - jnp.einsum("bp,bpuv->puv", coef_imag, crop_imag)
        exit_imag = jnp.einsum("bp,bpuv->puv", coef_real, crop_imag) + jnp.einsum("bp,bpuv->puv", coef_imag, crop_real)
        return exit_real, exit_imag

    blocks = (beam_index.reshape(-1, BEAM_DEV, 2), beam_weight.reshape(-1, BEAM_DEV))
    parts_real, parts_imag = lax.map(one_block, blocks)
    total_real = jnp.sum(parts_real, axis=0)
    total_imag = jnp.sum(parts_imag, axis=0)
    intensity = (total_real * total_real + total_imag * total_imag) / beam_weight.shape[0]
    return intensity.reshape(probe_total, CROP * CROP)
```

```python
import functools
import math

import jax
import jax.numpy as jnp
import numpy as np
from jax import lax
from jax.experimental import pallas as pl
from jax.experimental.pallas import tpu as pltpu
from jax.sharding import PartitionSpec as P

CROP = 16
REACH = 5
HALO = 16
CENTRE = 1.2
F32 = jnp.float32
BF16 = jnp.bfloat16


def make_taps():
    offsets = np.arange(-REACH, REACH + 1, dtype=np.float64)
    blur = np.exp(-(offsets**2) / 4.5)
    blur = blur / blur.sum()
    weight = np.exp(-(offsets**2) / 18.0)
    weight = weight / weight.sum()
    spread = weight * np.exp(1j * 0.35 * offsets**2)
    return blur, spread


def fit(function, limit, terms):
    nodes = 0.5 * limit * (1.0 + np.cos(np.pi * (np.arange(64) + 0.5) / 64))
    return np.polynomial.Polynomial.fit(nodes, function(nodes), terms - 1, domain=[0, limit]).convert().coef


def horner(coefs, x):
    result = jnp.full_like(x, float(coefs[-1]))
    for coef in coefs[-2::-1]:
        result = result * x + float(coef)
    return result


def cos_sin_small(t):
    square = t * t
    root = np.sqrt
    even = fit(lambda s: np.cos(root(s)), 1.69, 6)
    odd = fit(lambda s: np.sin(root(s)) / root(s), 1.69, 5)
    return horner(even, square), t * horner(odd, square)


def cos_sin_turns(turns):
    turns = turns - jnp.floor(turns + 0.5)
    square = turns * turns
    full = lambda s: 2.0 * np.pi * np.sqrt(s)
    even = fit(lambda s: np.cos(full(s)), 0.25, 9)
    odd = fit(lambda s: np.sin(full(s)) / np.sqrt(s), 0.25, 8)
    return horner(even, square), turns * horner(odd, square)


def band(distance, values):
    result = jnp.zeros(distance.shape, F32)
    reach = jnp.abs(distance)
    for k in range(REACH + 1):
        result = jnp.where(reach == k, float(values[REACH + k]), result)
    return result


def split(x):
    high = x.astype(BF16)
    return high, (x - high.astype(F32)).astype(BF16)


def blur_matrix(shift):
    blur, _ = make_taps()
    rows = lax.broadcasted_iota(jnp.int32, (128, 128), 0)
    cols = lax.broadcasted_iota(jnp.int32, (128, 128), 1)
    values = band(rows - cols - shift - REACH, 0.6 * blur)
    high, low = split(jnp.where(rows // 64 == cols // 64, values, 0.0))
    return jnp.concatenate([high, low], axis=1)


def spread_matrix():
    _, spread = make_taps()
    turned = spread * np.exp(1j * CENTRE)
    rows = lax.broadcasted_iota(jnp.int32, (128, 128), 0)
    cols = lax.broadcasted_iota(jnp.int32, (128, 128), 1)
    same = rows // 64 == cols // 64
    distance = rows - cols - REACH
    real = jnp.where(same, band(distance, turned.real), 0.0)
    imag = jnp.where(same, band(distance, turned.imag), 0.0)
    whole = jnp.concatenate(
        [jnp.concatenate([real, imag], axis=1), jnp.concatenate([-imag, real], axis=1)], axis=0
    )
    return split(whole)


def dot(a, b):
    return jnp.dot(a, b, preferred_element_type=F32)


def dot3(x, high, low):
    x_high, x_low = split(x)
    return dot(x_high, high) + dot(x_low, high) + dot(x_high, low)


def blur_rows(x):
    blur, _ = make_taps()
    rows = x.shape[0] - 2 * REACH
    result = float(blur[REACH]) * x[REACH : REACH + rows]
    for k in range(REACH):
        far = 2 * REACH - k
        result = result + float(blur[k]) * (x[k : k + rows] + x[far : far + rows])
    return result


def spread_rows(real, imag):
    _, spread = make_taps()
    rows = real.shape[0] - 2 * REACH
    out_real, out_imag = 0.0, 0.0
    for k in range(REACH + 1):
        near, far = k, 2 * REACH - k
        a, b = real[near : near + rows], imag[near : near + rows]
        if near != far:
            a, b = a + real[far : far + rows], b + imag[far : far + rows]
        c, s = float(spread[k].real), float(spread[k].imag)
        out_real = out_real + (c * a - s * b)
        out_imag = out_imag + (c * b + s * a)
    return out_real, out_imag


def place_rows(ext, source, first, extent):
    slices, rows, cols = source.shape
    tiles = cols // 128

    def one(tile, carry):
        for s in range(slices):
            block = source[s, :, pl.ds(pl.multiple_of(tile * 128, 128), 128)]
            start = pl.multiple_of((s * tiles + tile) * extent + first, 16)
            ext[pl.ds(start, rows), :] = block.astype(F32)
        return carry

    lax.fori_loop(0, tiles, one, 0, unroll=4)


def take_windows(ext, extent, tiles, probe_rows, probe_cols, gathered, slice_index, first, row_count, u, half):
    cols_total = tiles * 128
    pairs = probe_rows.shape[0] // 2
    lane = lax.broadcasted_iota(jnp.int32, (row_count, 128), 1)

    def window(probe, place):
        start = lax.rem(probe_cols[probe] + 8 * half - 3 * REACH + cols_total, cols_total)
        tile, offset = start // 128, lax.rem(start, 128)
        after = lax.rem(tile + 1, tiles)
        row = probe_rows[probe] + u + first
        near = ext[pl.ds((slice_index * tiles + tile) * extent + row, row_count), :]
        far = ext[pl.ds((slice_index * tiles + after) * extent + row, row_count), :]
        both = jnp.where(lane >= offset, near, far)
        return pltpu.roll(both, lax.rem(128 - offset + place, 128), 1)

    def one(pair, carry):
        joined = jnp.where(lane < 64, window(pair, 0), window(pair + pairs, 64))
        gathered[pl.ds(pair, row_count, stride=pairs), :] = joined
        return carry

    lax.fori_loop(0, pairs, one, 0, unroll=4)


def transmission(gathered, shift):
    pairs = 32
    blurred = dot(gathered[...].astype(BF16), blur_matrix(shift))
    blurred = blurred[:, :128] + blurred[:, 128:]
    rows = blurred.reshape(gathered.shape[0] // pairs, pairs, 128)
    rows = rows[: rows.shape[0] - (1 if shift == 0 else 3)]
    return cos_sin_small(blur_rows(rows) - CENTRE)


def probe_function(table, u, half):
    kx, ky, weight = table[:, 0:1], table[:, 1:2], table[:, 2:3]
    lane = lax.broadcasted_iota(jnp.int32, (table.shape[0], 128), 1)
    down = (lane + (u - 2 * REACH)).astype(F32)
    across = (lax.rem(lane, 64) + (8 * half - 2 * REACH)).astype(F32)
    row_cos, row_sin = cos_sin_turns(kx * down * (1.0 / 512.0))
    col_cos, col_sin = cos_sin_turns(ky * across * (1.0 / 4096.0))
    left = jnp.concatenate([weight * row_cos, weight * row_sin], axis=0)
    right = jnp.concatenate(
        [
            jnp.concatenate([col_cos, col_sin], axis=1),
            jnp.concatenate([-col_sin, col_cos], axis=1),
        ],
        axis=0,
    )
    return lax.dot_general(
        left, right, (((0,), (0,)), ((), ())), precision=lax.Precision.HIGHEST,
        preferred_element_type=F32,
    )


def propagate(wave, first_cos, first_sin, second_cos, second_sin, beams):
    pairs = first_cos.shape[1]
    high, low = spread_matrix()
    rows = first_cos.shape[0]
    wave_real = wave[:rows, None, :128]
    wave_imag = wave[:rows, None, 128:]
    real = first_cos * wave_real - first_sin * wave_imag
    imag = first_cos * wave_imag + first_sin * wave_real
    real, imag = spread_rows(real, imag)
    rows = real.shape[0]
    both = jnp.concatenate([real, imag], axis=2).reshape(rows * pairs, 256)
    both = dot3(both, high, low).reshape(rows, pairs, 256)
    real, imag = both[:, :, :128], both[:, :, 128:]
    real, imag = real * second_cos - imag * second_sin, real * second_sin + imag * second_cos
    real, imag = spread_rows(real, imag)
    both = dot3(jnp.concatenate([real[0], imag[0]], axis=1), high, low)
    return (both[:, :128] * both[:, :128] + both[:, 128:] * both[:, 128:]) * (1.0 / beams)


def kernel(probe_rows, probe_cols, own, prev, following, table, out, ext, first, second):
    beam = lax.axis_index("beam")
    u, half = beam // 2, lax.rem(beam, 2)
    strip = own.shape[1]
    tiles = own.shape[2] // 128
    extent = strip + 2 * HALO
    place_rows(ext, prev, 0, extent)
    place_rows(ext, own, HALO, extent)
    place_rows(ext, following, HALO + strip, extent)
    take_windows(ext, extent, tiles, probe_rows, probe_cols, first, 0, 1, 32, u, half)
    take_windows(ext, extent, tiles, probe_rows, probe_cols, second, 1, 6, 24, u, half)
    first_cos, first_sin = transmission(first, 0)
    second_cos, second_sin = transmission(second, REACH)
    wave = probe_function(table[...], u, half)
    result = propagate(wave, first_cos, first_sin, second_cos, second_sin, table.shape[0])
    out[0:32, :] = result[:, 0:8]
    out[32:64, :] = result[:, 64:72]


def body(atom_counts, beam_index, beam_weight, probe_rows, probe_cols):
    slices, strip, cols = atom_counts.shape
    count = lax.axis_size("tile")
    forward = [(i, (i + 1) % count) for i in range(count)]
    backward = [(j, i) for i, j in forward]
    prev = lax.ppermute(atom_counts[:, strip - HALO :], "tile", forward)
    following = lax.ppermute(atom_counts[:, :HALO], "tile", backward)
    row = jnp.concatenate([beam_index.astype(F32), beam_weight[:, None]], axis=1)
    table = lax.all_gather(jnp.pad(row, ((0, 0), (0, 125))), "beam", axis=0, tiled=True)
    smem = pl.BlockSpec(memory_space=pltpu.SMEM)
    vmem = pl.BlockSpec(memory_space=pltpu.VMEM)
    return pl.pallas_call(
        kernel,
        out_shape=jax.ShapeDtypeStruct((probe_rows.shape[0], 8), F32),
        in_specs=[smem, smem, vmem, vmem, vmem, vmem],
        out_specs=vmem,
        scratch_shapes=[
            pltpu.VMEM((slices * (strip + 2 * HALO) * cols // 128, 128), F32),
            pltpu.VMEM((32 * 32, 128), F32),
            pltpu.VMEM((24 * 32, 128), F32),
        ],
        compiler_params=pltpu.CompilerParams(vmem_limit_bytes=40 * 2**20),
    )(probe_rows, probe_cols, atom_counts, prev, following, table)


def solution(mesh):
    return jax.shard_map(
        body,
        mesh=mesh,
        in_specs=(P(None, "tile", None), P("beam", None), P("beam"), P("tile"), P("tile")),
        out_specs=P("tile", "beam"),
        check_vma=False,
    )
```

```python
import functools
import math

import jax
import jax.numpy as jnp
import numpy as np
from jax import lax
from jax.experimental import pallas as pl
from jax.experimental.pallas import tpu as pltpu
from jax.sharding import PartitionSpec as P

CROP = 16
REACH = 5
HALO = 16
CENTRE = 1.2
F32 = jnp.float32
BF16 = jnp.bfloat16
MESH = pl.DeviceIdType.MESH


def make_taps():
    offsets = np.arange(-REACH, REACH + 1, dtype=np.float64)
    blur = np.exp(-(offsets**2) / 4.5)
    blur = blur / blur.sum()
    weight = np.exp(-(offsets**2) / 18.0)
    weight = weight / weight.sum()
    spread = weight * np.exp(1j * 0.35 * offsets**2)
    return blur, spread


def fit(function, limit, terms):
    nodes = 0.5 * limit * (1.0 + np.cos(np.pi * (np.arange(64) + 0.5) / 64))
    return np.polynomial.Polynomial.fit(nodes, function(nodes), terms - 1, domain=[0, limit]).convert().coef


def horner(coefs, x):
    result = jnp.full_like(x, float(coefs[-1]))
    for coef in coefs[-2::-1]:
        result = result * x + float(coef)
    return result


def cos_sin_small(t):
    square = t * t
    root = np.sqrt
    even = fit(lambda s: np.cos(root(s)), 1.69, 6)
    odd = fit(lambda s: np.sin(root(s)) / root(s), 1.69, 5)
    return horner(even, square), t * horner(odd, square)


def cos_sin_turns(turns):
    turns = turns - jnp.floor(turns + 0.5)
    square = turns * turns
    full = lambda s: 2.0 * np.pi * np.sqrt(s)
    even = fit(lambda s: np.cos(full(s)), 0.25, 9)
    odd = fit(lambda s: np.sin(full(s)) / np.sqrt(s), 0.25, 8)
    return horner(even, square), turns * horner(odd, square)


def band(distance, values):
    result = jnp.zeros(distance.shape, F32)
    reach = jnp.abs(distance)
    for k in range(REACH + 1):
        result = jnp.where(reach == k, float(values[REACH + k]), result)
    return result


def split(x):
    high = x.astype(BF16)
    return high, (x - high.astype(F32)).astype(BF16)


def blur_matrix(shift):
    blur, _ = make_taps()
    rows = lax.broadcasted_iota(jnp.int32, (128, 128), 0)
    cols = lax.broadcasted_iota(jnp.int32, (128, 128), 1)
    values = band(rows - cols - shift - REACH, 0.6 * blur)
    high, low = split(jnp.where(rows // 64 == cols // 64, values, 0.0))
    return jnp.concatenate([high, low], axis=1)


def spread_matrix():
    _, spread = make_taps()
    turned = spread * np.exp(1j * CENTRE)
    rows = lax.broadcasted_iota(jnp.int32, (128, 128), 0)
    cols = lax.broadcasted_iota(jnp.int32, (128, 128), 1)
    same = rows // 64 == cols // 64
    distance = rows - cols - REACH
    real = jnp.where(same, band(distance, turned.real), 0.0)
    imag = jnp.where(same, band(distance, turned.imag), 0.0)
    whole = jnp.concatenate(
        [jnp.concatenate([real, imag], axis=1), jnp.concatenate([-imag, real], axis=1)], axis=0
    )
    return split(whole)


def dot(a, b):
    return jnp.dot(a, b, preferred_element_type=F32)


def dot3(x, high, low):
    x_high, x_low = split(x)
    return dot(x_high, high) + dot(x_low, high) + dot(x_high, low)


def blur_rows(x):
    blur, _ = make_taps()
    rows = x.shape[0] - 2 * REACH
    result = float(blur[REACH]) * x[REACH : REACH + rows]
    for k in range(REACH):
        far = 2 * REACH - k
        result = result + float(blur[k]) * (x[k : k + rows] + x[far : far + rows])
    return result


def spread_rows(real, imag):
    _, spread = make_taps()
    rows = real.shape[0] - 2 * REACH
    out_real, out_imag = 0.0, 0.0
    for k in range(REACH + 1):
        near, far = k, 2 * REACH - k
        a, b = real[near : near + rows], imag[near : near + rows]
        if near != far:
            a, b = a + real[far : far + rows], b + imag[far : far + rows]
        c, s = float(spread[k].real), float(spread[k].imag)
        out_real = out_real + (c * a - s * b)
        out_imag = out_imag + (c * b + s * a)
    return out_real, out_imag


def place_rows(ext, source, first, extent):
    slices, rows, cols = source.shape
    tiles = cols // 128

    def one(tile, carry):
        for s in range(slices):
            block = source[s, :, pl.ds(pl.multiple_of(tile * 128, 128), 128)]
            start = pl.multiple_of((s * tiles + tile) * extent + first, 16)
            ext[pl.ds(start, rows), :] = block.astype(F32)
        return carry

    lax.fori_loop(0, tiles, one, 0, unroll=4)


def place_halo(ext, halo, s, extent, strip):
    tiles = halo.shape[3] // 128

    def one(tile, carry):
        for side, first in ((0, 0), (1, HALO + strip)):
            block = halo[side, s, :, pl.ds(pl.multiple_of(tile * 128, 128), 128)]
            start = pl.multiple_of((s * tiles + tile) * extent + first, 16)
            ext[pl.ds(start, HALO), :] = block.astype(F32)
        return carry

    lax.fori_loop(0, tiles, one, 0, unroll=4)


def take_windows(ext, extent, tiles, probe_rows, probe_cols, gathered, slice_index, first, row_count, u, half):
    cols_total = tiles * 128
    pairs = probe_rows.shape[0] // 2
    lane = lax.broadcasted_iota(jnp.int32, (row_count, 128), 1)

    def window(probe, place):
        start = lax.rem(probe_cols[probe] + 8 * half - 3 * REACH + cols_total, cols_total)
        tile, offset = start // 128, lax.rem(start, 128)
        after = lax.rem(tile + 1, tiles)
        row = probe_rows[probe] + u + first
        near = ext[pl.ds((slice_index * tiles + tile) * extent + row, row_count), :]
        far = ext[pl.ds((slice_index * tiles + after) * extent + row, row_count), :]
        both = jnp.where(lane >= offset, near, far)
        return pltpu.roll(both, lax.rem(128 - offset + place, 128), 1)

    def one(pair, carry):
        joined = jnp.where(lane < 64, window(pair, 0), window(pair + pairs, 64))
        gathered[pl.ds(pair, row_count, stride=pairs), :] = joined
        return carry

    lax.fori_loop(0, pairs, one, 0, unroll=4)


def transmission(gathered, shift):
    pairs = 32
    blurred = dot(gathered[...].astype(BF16), blur_matrix(shift))
    blurred = blurred[:, :128] + blurred[:, 128:]
    rows = blurred.reshape(gathered.shape[0] // pairs, pairs, 128)
    rows = rows[: rows.shape[0] - (1 if shift == 0 else 3)]
    return cos_sin_small(blur_rows(rows) - CENTRE)


def probe_function(table, u, half):
    kx, ky, weight = table[:, 0:1], table[:, 1:2], table[:, 2:3]
    lane = lax.broadcasted_iota(jnp.int32, (table.shape[0], 128), 1)
    down = (lane + (u - 2 * REACH)).astype(F32)
    across = (lax.rem(lane, 64) + (8 * half - 2 * REACH)).astype(F32)
    row_cos, row_sin = cos_sin_turns(kx * down * (1.0 / 512.0))
    col_cos, col_sin = cos_sin_turns(ky * across * (1.0 / 4096.0))
    left = jnp.concatenate([weight * row_cos, weight * row_sin], axis=0)
    right = jnp.concatenate(
        [
            jnp.concatenate([col_cos, col_sin], axis=1),
            jnp.concatenate([-col_sin, col_cos], axis=1),
        ],
        axis=0,
    )
    return lax.dot_general(
        left, right, (((0,), (0,)), ((), ())), precision=lax.Precision.HIGHEST,
        preferred_element_type=F32,
    )


def propagate(wave, first_cos, first_sin, second_cos, second_sin, beams):
    pairs = first_cos.shape[1]
    high, low = spread_matrix()
    rows = first_cos.shape[0]
    wave_real = wave[:rows, None, :128]
    wave_imag = wave[:rows, None, 128:]
    real = first_cos * wave_real - first_sin * wave_imag
    imag = first_cos * wave_imag + first_sin * wave_real
    real, imag = spread_rows(real, imag)
    rows = real.shape[0]
    both = jnp.concatenate([real, imag], axis=2).reshape(rows * pairs, 256)
    both = dot3(both, high, low).reshape(rows, pairs, 256)
    real, imag = both[:, :, :128], both[:, :, 128:]
    real, imag = real * second_cos - imag * second_sin, real * second_sin + imag * second_cos
    real, imag = spread_rows(real, imag)
    both = dot3(jnp.concatenate([real[0], imag[0]], axis=1), high, low)
    return (both[:, :128] * both[:, :128] + both[:, 128:] * both[:, 128:]) * (1.0 / beams)


def kernel(
    probe_rows, probe_cols, beam_index, beam_weight, counts, out,
    own, halo, table, ext, first, second,
    own_sem, halo_send, halo_recv, share_send, share_recv, row_send, row_recv,
    table_send, table_recv, ready,
):
    beam, tile = lax.axis_index("beam"), lax.axis_index("tile")
    tiles_total = lax.axis_size("tile")
    group = 8
    lines = lax.axis_size("beam") // group
    half_tiles = tiles_total // 2
    x, place = beam // group, lax.rem(beam, group)
    early = tile < half_tiles
    across_up = lax.rem(tile, half_tiles) == half_tiles - 1
    across_down = lax.rem(tile, half_tiles) == 0
    mirrored = x * group + (group - 1 - place)
    up = (jnp.where(across_up, mirrored, beam), lax.rem(tile + 1, tiles_total))
    down = (jnp.where(across_down, mirrored, beam), lax.rem(tile + tiles_total - 1, tiles_total))
    other_half = (beam, lax.rem(tile + half_tiles, tiles_total))
    slices, strip, cols = own.shape
    part = cols // lines

    def member(line, z):
        return line * group + z

    own_copy = pltpu.make_async_copy(counts, own, own_sem)
    own_copy.start()

    barrier = pltpu.get_barrier_semaphore()

    def tell(device):
        pl.semaphore_signal(barrier, inc=1, device_id=device, device_id_type=MESH)

    for step in range(1, lines):
        tell((member(lax.rem(x + step, lines), place), tile))
    for device, across in ((up, across_up), (down, across_down)):

        @pl.when(jnp.logical_or(early, jnp.logical_not(across)))
        def _():
            tell(device)

    @pl.when(early)
    def _():
        tell(other_half)

        def tell_later(z, carry):
            for line in range(lines):
                tell((member(line, z), tile))
            return carry

        lax.fori_loop(place + 1, group, tell_later, 0)

    lane = lax.broadcasted_iota(jnp.int32, (1, 128), 1)

    @pl.when(early)
    def _():
        kx = beam_index[0, 0].astype(F32)
        ky = beam_index[0, 1].astype(F32)
        table[beam] = jnp.where(
            lane == 0, kx, jnp.where(lane == 1, ky, jnp.where(lane == 2, beam_weight[0], 0.0))
        )

    across_any = jnp.logical_or(across_up, across_down).astype(jnp.int32)
    expected = (lines - 1) + 2 - across_any
    expected = expected + jnp.where(early, lines * place, 1 + across_any)
    pl.semaphore_wait(barrier, expected)

    def row_copy(peer):
        return pltpu.make_async_remote_copy(
            src_ref=table.at[beam], dst_ref=table.at[beam], send_sem=row_send.at[peer],
            recv_sem=row_recv.at[beam], device_id=(peer, tile), device_id_type=MESH,
        )

    def row_arrival(peer):
        return pltpu.make_async_remote_copy(
            src_ref=table.at[peer], dst_ref=table.at[peer], send_sem=row_send.at[peer],
            recv_sem=row_recv.at[peer], device_id=(peer, tile), device_id_type=MESH,
        )

    table_copy = pltpu.make_async_remote_copy(
        src_ref=table, dst_ref=table, send_sem=table_send, recv_sem=table_recv,
        device_id=other_half, device_id_type=MESH,
    )

    @pl.when(early)
    def _():
        for step in range(1, lines):
            row_copy(member(lax.rem(x + step, lines), place)).start()

        def send_back(z, carry):
            for line in range(lines):
                row_copy(member(line, z)).start()
            return carry

        lax.fori_loop(0, place, send_back, 0)

    @pl.when(jnp.logical_not(early))
    def _():
        pl.semaphore_signal(ready, inc=1, device_id=other_half, device_id_type=MESH)

    my_part = pl.ds(pl.multiple_of(x * part, part), part)

    def halo_copy(side, s):
        rows = pl.ds(strip - HALO, HALO) if side == 0 else pl.ds(0, HALO)
        return pltpu.make_async_remote_copy(
            src_ref=own.at[s, rows, my_part], dst_ref=halo.at[side, s, :, my_part],
            send_sem=halo_send.at[side, s], recv_sem=halo_recv.at[side, s],
            device_id=up if side == 0 else down, device_id_type=MESH,
        )

    def share_copy(side, s, step):
        return pltpu.make_async_remote_copy(
            src_ref=halo.at[side, s, :, my_part], dst_ref=halo.at[side, s, :, my_part],
            send_sem=share_send.at[side, s, step - 1], recv_sem=share_recv.at[side, s, step - 1],
            device_id=(member(lax.rem(x + step, lines), place), tile), device_id_type=MESH,
        )

    def share_arrival(side, s, step):
        theirs = lax.rem(x + lines - step, lines)
        where = pl.ds(pl.multiple_of(theirs * part, part), part)
        return pltpu.make_async_remote_copy(
            src_ref=halo.at[side, s, :, where], dst_ref=halo.at[side, s, :, where],
            send_sem=share_send.at[side, s, step - 1], recv_sem=share_recv.at[side, s, step - 1],
            device_id=(member(theirs, place), tile), device_id_type=MESH,
        )

    own_copy.wait()
    for s in range(slices):
        for side, across in ((0, across_up), (1, across_down)):

            @pl.when(jnp.logical_not(jnp.logical_and(early, across)))
            def _():
                halo_copy(side, s).start()

    extent = strip + 2 * HALO
    place_rows(ext, own, HALO, extent)

    for s in range(slices):
        for side, across in ((0, across_down), (1, across_up)):
            halo_copy(side, s).wait_recv()

            @pl.when(jnp.logical_and(early, across))
            def _():
                halo_copy(1 - side, s).start()

            for step in range(1, lines):
                share_copy(side, s, step).start()

    @pl.when(early)
    def _():
        def answer(z, carry):
            for line in range(lines):
                peer = member(line, z)
                row_arrival(peer).wait_recv()
                row_copy(peer).start()
            return carry

        lax.fori_loop(place + 1, group, answer, 0)
        for step in range(1, lines):
            row_arrival(member(lax.rem(x + step, lines), place)).wait_recv()

        def collect(z, carry):
            for line in range(lines):
                row_arrival(member(line, z)).wait_recv()
            return carry

        lax.fori_loop(0, place, collect, 0)
        pl.semaphore_wait(ready, 1)
        table_copy.start()

    @pl.when(jnp.logical_not(early))
    def _():
        table_copy.wait_recv()

    u, half = beam // 2, lax.rem(beam, 2)
    tiles = cols // 128
    wave = probe_function(table[:, 0, :], u, half)

    parts = []
    for s, (gathered, row, count, shift) in enumerate(
        ((first, 1, 32, 0), (second, 6, 24, REACH))
    ):
        for side in (0, 1):
            for step in range(1, lines):
                share_arrival(side, s, step).wait_recv()
        place_halo(ext, halo, s, extent, strip)
        take_windows(ext, extent, tiles, probe_rows, probe_cols, gathered, s, row, count, u, half)
        parts.extend(transmission(gathered, shift))
    result = propagate(wave, *parts, table.shape[0])
    turned = jnp.transpose(result)
    out[:, 0:32] = turned[0:8]
    out[:, 32:64] = turned[64:72]

    for s in range(slices):
        for side in (0, 1):
            halo_copy(side, s).wait_send()
            for step in range(1, lines):
                share_copy(side, s, step).wait_send()

    @pl.when(early)
    def _():
        table_copy.wait_send()

        def sent(step, carry):
            row_copy(lax.rem(beam + step, lines * group)).wait_send()
            return carry

        lax.fori_loop(1, lines * group, sent, 0)


def body(atom_counts, beam_index, beam_weight, probe_rows, probe_cols):
    slices, strip, cols = atom_counts.shape
    beams = lax.axis_size("beam")
    lines = beams // 8
    smem = pl.BlockSpec(memory_space=pltpu.SMEM)
    dma = pltpu.SemaphoreType.DMA
    result = pl.pallas_call(
        kernel,
        out_shape=jax.ShapeDtypeStruct((8, probe_rows.shape[0]), F32),
        in_specs=[smem, smem, smem, smem, pl.BlockSpec(memory_space=pltpu.HBM)],
        out_specs=pl.BlockSpec(memory_space=pltpu.VMEM),
        scratch_shapes=[
            pltpu.VMEM((slices, strip, cols), BF16),
            pltpu.VMEM((2, slices, HALO, cols), BF16),
            pltpu.VMEM((beams, 1, 128), F32),
            pltpu.VMEM((slices * (strip + 2 * HALO) * cols // 128, 128), F32),
            pltpu.VMEM((32 * 32, 128), F32),
            pltpu.VMEM((24 * 32, 128), F32),
            dma(()),
            dma((2, slices)),
            dma((2, slices)),
            dma((2, slices, lines - 1)),
            dma((2, slices, lines - 1)),
            dma((beams,)),
            dma((beams,)),
            dma(()),
            dma(()),
            pltpu.SemaphoreType.REGULAR,
        ],
        compiler_params=pltpu.CompilerParams(
            collective_id=0, has_side_effects=True, vmem_limit_bytes=40 * 2**20
        ),
    )(probe_rows, probe_cols, beam_index, beam_weight, atom_counts)
    return result.T


def solution(mesh):
    return jax.shard_map(
        body,
        mesh=mesh,
        in_specs=(P(None, "tile", None), P("beam", None), P("beam"), P("tile"), P("tile")),
        out_specs=P("tile", "beam"),
        check_vma=False,
    )
```

```python
import functools
import math

import jax
import jax.numpy as jnp
import numpy as np
from jax import lax
from jax.experimental import pallas as pl
from jax.experimental.pallas import tpu as pltpu
from jax.sharding import PartitionSpec as P

CROP = 16
REACH = 5
HALO = 16
CENTRE = 1.2
F32 = jnp.float32
BF16 = jnp.bfloat16
MESH = pl.DeviceIdType.MESH


def make_taps():
    offsets = np.arange(-REACH, REACH + 1, dtype=np.float64)
    blur = np.exp(-(offsets**2) / 4.5)
    blur = blur / blur.sum()
    weight = np.exp(-(offsets**2) / 18.0)
    weight = weight / weight.sum()
    spread = weight * np.exp(1j * 0.35 * offsets**2)
    return blur, spread


def fit(function, limit, terms):
    nodes = 0.5 * limit * (1.0 + np.cos(np.pi * (np.arange(64) + 0.5) / 64))
    return np.polynomial.Polynomial.fit(nodes, function(nodes), terms - 1, domain=[0, limit]).convert().coef


def horner(coefs, x):
    result = jnp.full_like(x, float(coefs[-1]))
    for coef in coefs[-2::-1]:
        result = result * x + float(coef)
    return result


def cos_sin_small(t):
    square = t * t
    root = np.sqrt
    even = fit(lambda s: np.cos(root(s)), 1.69, 6)
    odd = fit(lambda s: np.sin(root(s)) / root(s), 1.69, 5)
    return horner(even, square), t * horner(odd, square)


def cos_sin_turns(turns):
    turns = turns - jnp.floor(turns + 0.5)
    square = turns * turns
    full = lambda s: 2.0 * np.pi * np.sqrt(s)
    even = fit(lambda s: np.cos(full(s)), 0.25, 9)
    odd = fit(lambda s: np.sin(full(s)) / np.sqrt(s), 0.25, 8)
    return horner(even, square), turns * horner(odd, square)


def band(distance, values):
    result = jnp.zeros(distance.shape, F32)
    reach = jnp.abs(distance)
    for k in range(REACH + 1):
        result = jnp.where(reach == k, float(values[REACH + k]), result)
    return result


def split(x):
    high = x.astype(BF16)
    return high, (x - high.astype(F32)).astype(BF16)


def blur_matrix(shift):
    blur, _ = make_taps()
    rows = lax.broadcasted_iota(jnp.int32, (128, 128), 0)
    cols = lax.broadcasted_iota(jnp.int32, (128, 128), 1)
    values = band(rows - cols - shift - REACH, 0.6 * blur)
    high, low = split(jnp.where(rows // 64 == cols // 64, values, 0.0))
    return jnp.concatenate([high, low], axis=1)


def spread_matrix():
    _, spread = make_taps()
    turned = spread * np.exp(1j * CENTRE)
    rows = lax.broadcasted_iota(jnp.int32, (128, 128), 0)
    cols = lax.broadcasted_iota(jnp.int32, (128, 128), 1)
    same = rows // 64 == cols // 64
    distance = rows - cols - REACH
    real = jnp.where(same, band(distance, turned.real), 0.0)
    imag = jnp.where(same, band(distance, turned.imag), 0.0)
    whole = jnp.concatenate(
        [jnp.concatenate([real, imag], axis=1), jnp.concatenate([-imag, real], axis=1)], axis=0
    )
    return split(whole)


def dot(a, b):
    return jnp.dot(a, b, preferred_element_type=F32)


def dot3(x, high, low):
    x_high, x_low = split(x)
    return dot(x_high, high) + dot(x_low, high) + dot(x_high, low)


def place_rows(ext, source, first, extent):
    slices, rows, cols = source.shape
    tiles = cols // 128

    def one(tile, carry):
        for s in range(slices):
            block = source[s, :, pl.ds(pl.multiple_of(tile * 128, 128), 128)]
            start = pl.multiple_of((s * tiles + tile) * extent + first, 16)
            ext[pl.ds(start, rows), :] = block.astype(F32)
        return carry

    lax.fori_loop(0, tiles, one, 0, unroll=8)


def place_halo(ext, halo, s, extent, strip):
    tiles = halo.shape[3] // 128

    def one(tile, carry):
        for side, first in ((0, 0), (1, HALO + strip)):
            block = halo[side, s, :, pl.ds(pl.multiple_of(tile * 128, 128), 128)]
            start = pl.multiple_of((s * tiles + tile) * extent + first, 16)
            ext[pl.ds(start, HALO), :] = block.astype(F32)
        return carry

    lax.fori_loop(0, tiles, one, 0, unroll=8)


def take_windows(ext, extent, tiles, rows, cols, gathered, slice_index, first, count, u, half):
    cols_total = tiles * 128
    pairs = rows.shape[0] // 2
    lane = lax.broadcasted_iota(jnp.int32, (count, 128), 1)

    def window(probe, place):
        start = lax.rem(cols[probe] + (8 * half - 3 * REACH + cols_total), cols_total)
        tile, offset = start >> 7, start & 127
        after = lax.rem(tile + 1, tiles)
        row = rows[probe] + (u + first)
        near = ext[pl.ds((slice_index * tiles + tile) * extent + row, count), :]
        far = ext[pl.ds((slice_index * tiles + after) * extent + row, count), :]
        both = jnp.where(lane >= offset, near, far)
        return pltpu.roll(both, (128 - offset + place) & 127, 1)

    def one(pair, carry):
        joined = jnp.where(lane < 64, window(pair, 0), window(pair + pairs, 64))
        gathered[pl.ds(pair, count, stride=pairs), :] = joined
        return carry

    lax.fori_loop(0, pairs, one, 0, unroll=16)


def row_at(i, k):
    return pl.ds(pl.multiple_of((i + k) * 32, 32), 32)


def transmission(gathered, blurred, matrix, trans):
    blur, _ = make_taps()
    both = dot(gathered[...].astype(BF16), matrix[...])
    blurred[0 : gathered.shape[0], :] = both[:, :128] + both[:, 128:]

    def one(i, carry):
        total = float(blur[REACH]) * blurred[row_at(i, REACH), :] - CENTRE
        for k in range(REACH):
            near, far = blurred[row_at(i, k), :], blurred[row_at(i, 2 * REACH - k), :]
            total = total + float(blur[k]) * (near + far)
        trans[0, row_at(i, 0), :], trans[1, row_at(i, 0), :] = cos_sin_small(total)
        return carry

    rows = trans.shape[1] // 32
    lax.fori_loop(0, rows, one, 0, unroll=rows)


def spread_rows(psi, i):
    _, spread = make_taps()
    out_real, out_imag = None, None
    for k in range(REACH + 1):
        a, b = psi[0, row_at(i, k), :], psi[1, row_at(i, k), :]
        if k != REACH:
            a = a + psi[0, row_at(i, 2 * REACH - k), :]
            b = b + psi[1, row_at(i, 2 * REACH - k), :]
        c, s = float(spread[k].real), float(spread[k].imag)
        real, imag = c * a - s * b, c * b + s * a
        out_real = real if out_real is None else out_real + real
        out_imag = imag if out_imag is None else out_imag + imag
    return out_real, out_imag


def probe_function(table, u, half):
    kx, ky, weight = table[:, 0:1], table[:, 1:2], table[:, 2:3]
    lane = lax.broadcasted_iota(jnp.int32, (table.shape[0], 128), 1)
    down = (lane + (u - 2 * REACH)).astype(F32)
    across = (lax.rem(lane, 64) + (8 * half - 2 * REACH)).astype(F32)
    row_cos, row_sin = cos_sin_turns(kx * down * (1.0 / 512.0))
    col_cos, col_sin = cos_sin_turns(ky * across * (1.0 / 4096.0))
    left = jnp.concatenate([weight * row_cos, weight * row_sin], axis=0)
    right = jnp.concatenate(
        [
            jnp.concatenate([col_cos, col_sin], axis=1),
            jnp.concatenate([-col_sin, col_cos], axis=1),
        ],
        axis=0,
    )
    return lax.dot_general(
        left, right, (((0,), (0,)), ((), ())), precision=lax.Precision.HIGHEST,
        preferred_element_type=F32,
    )


def propagate(wave_ref, trans0, trans1, psi, both, spread, beams):
    rows0, rows1 = trans0.shape[1] // 32, trans1.shape[1] // 32

    def enter(i, carry):
        cos, sin = trans0[0, row_at(i, 0), :], trans0[1, row_at(i, 0), :]
        real = wave_ref[pl.ds(i, 1), 0:128]
        imag = wave_ref[pl.ds(i, 1), 128:256]
        psi[0, row_at(i, 0), :] = cos * real - sin * imag
        psi[1, row_at(i, 0), :] = cos * imag + sin * real
        return carry

    lax.fori_loop(0, rows0, enter, 0, unroll=rows0)

    def between(i, carry):
        both[row_at(i, 0), 0:128], both[row_at(i, 0), 128:256] = spread_rows(psi, i)
        return carry

    lax.fori_loop(0, rows1, between, 0, unroll=rows1)
    both[...] = dot3(both[...], spread[0], spread[1])

    def again(i, carry):
        real, imag = both[row_at(i, 0), 0:128], both[row_at(i, 0), 128:256]
        cos, sin = trans1[0, row_at(i, 0), :], trans1[1, row_at(i, 0), :]
        psi[0, row_at(i, 0), :] = real * cos - imag * sin
        psi[1, row_at(i, 0), :] = real * sin + imag * cos
        return carry

    lax.fori_loop(0, rows1, again, 0, unroll=rows1)
    last = dot3(jnp.concatenate(spread_rows(psi, 0), axis=1), spread[0], spread[1])
    return (last[:, :128] * last[:, :128] + last[:, 128:] * last[:, 128:]) * (1.0 / beams)


def kernel(
    rows_hbm, cols_hbm, index_hbm, weight_hbm, counts, out,
    probe_rows, probe_cols, beam_index, beam_weight,
    own, halo, table, ext, first, second, blurred, matrix0, matrix1, spread,
    trans0, trans1, wave, psi, both,
    own_sem, small_sem, halo_send, halo_recv, share_send, share_recv, row_send, row_recv,
    table_send, table_recv, ready, hello, ready_edge,
):
    beam, tile = lax.axis_index("beam"), lax.axis_index("tile")
    tiles_total = lax.axis_size("tile")
    group = 8
    lines = lax.axis_size("beam") // group
    half_tiles = tiles_total // 2
    x, place = beam // group, lax.rem(beam, group)
    early = tile < half_tiles
    late = jnp.logical_not(early)
    across_up = lax.rem(tile, half_tiles) == half_tiles - 1
    across_down = lax.rem(tile, half_tiles) == 0
    across = jnp.logical_or(across_up, across_down)
    mirrored = x * group + (group - 1 - place)
    up = (jnp.where(across_up, mirrored, beam), lax.rem(tile + 1, tiles_total))
    down = (jnp.where(across_down, mirrored, beam), lax.rem(tile + tiles_total - 1, tiles_total))
    other_half = (mirrored, lax.rem(tile + half_tiles, tiles_total))
    slices, strip, cols = own.shape
    part = cols // lines
    on_first = tile == 0
    first_one = jnp.logical_and(on_first, beam == 0)
    skip_first = on_first.astype(jnp.int32)
    skip_line = jnp.logical_and(on_first, place == 0).astype(jnp.int32)

    def member(line, z):
        return line * group + z

    def slot(line, z):
        return z * lines + line

    def line_peer(step):
        return member(lax.rem(x + step, lines), place)

    my_part = pl.ds(pl.multiple_of(x * part, part), part)
    edge_rows = (pl.ds(strip - HALO, HALO), pl.ds(0, HALO))
    own_copies = [
        pltpu.make_async_copy(
            counts.at[s, edge_rows[side]], own.at[s, edge_rows[side]], own_sem.at[side, s]
        )
        for s in range(slices)
        for side in (0, 1)
    ]
    for copy in own_copies:
        copy.start()
    small_copies = [
        pltpu.make_async_copy(source, target, small_sem.at[k])
        for k, (source, target) in enumerate(
            (
                (index_hbm, beam_index), (weight_hbm, beam_weight),
                (rows_hbm, probe_rows), (cols_hbm, probe_cols),
            )
        )
    ]
    for copy in small_copies:
        copy.start()

    barrier = pltpu.get_barrier_semaphore()

    def tell(device):
        pl.semaphore_signal(barrier, inc=1, device_id=device, device_id_type=MESH)

    @pl.when(jnp.logical_and(on_first, beam > 0))
    def _():
        tell((0, 0))

    for device, far in ((up, across_up), (down, across_down)):

        @pl.when(jnp.logical_or(early, jnp.logical_not(far)))
        def _():
            tell(device)

    def tell_line(line, carry):
        tell((member(line, place), tile))
        return carry

    def tell_later(z, carry):
        for line in range(lines):
            tell((member(line, z), tile))
        return carry

    @pl.when(jnp.logical_not(first_one))
    def _():
        lax.fori_loop(x + 1, lines, tell_line, 0)

    @pl.when(early)
    def _():
        tell(other_half)

        @pl.when(jnp.logical_not(first_one))
        def _():
            lax.fori_loop(place + 1, group, tell_later, 0)


    lane = lax.broadcasted_iota(jnp.int32, (1, 128), 1)
    small_copies[0].wait()
    small_copies[1].wait()

    @pl.when(early)
    def _():
        kx = beam_index[0, 0].astype(F32)
        ky = beam_index[0, 1].astype(F32)
        table[slot(x, place)] = jnp.where(
            lane == 0, kx, jnp.where(lane == 1, ky, jnp.where(lane == 2, beam_weight[0], 0.0))
        )

    across_count = across.astype(jnp.int32)
    expected = x + jnp.where(early, lines * place, 1 + across_count) - skip_first
    expected = jnp.where(first_one, lines * group - 1, expected) + 2 - across_count
    pl.semaphore_wait(barrier, expected)

    my_slot = slot(x, place)

    def row_copy(line, z):
        return pltpu.make_async_remote_copy(
            src_ref=table.at[my_slot], dst_ref=table.at[my_slot], send_sem=row_send,
            recv_sem=row_recv.at[my_slot], device_id=(member(line, z), tile), device_id_type=MESH,
        )

    def row_arrival(line, z):
        theirs = slot(line, z)
        return pltpu.make_async_remote_copy(
            src_ref=table.at[theirs], dst_ref=table.at[theirs], send_sem=row_send,
            recv_sem=row_recv.at[theirs], device_id=(member(line, z), tile), device_id_type=MESH,
        )

    table_copy = pltpu.make_async_remote_copy(
        src_ref=table, dst_ref=table, send_sem=table_send, recv_sem=table_recv,
        device_id=other_half, device_id_type=MESH,
    )

    def send_line(line, carry):
        row_copy(line, place).start()
        return carry

    def send_all(z, carry):
        for line in range(lines):
            row_copy(line, z).start()
        return carry

    @pl.when(jnp.logical_and(early, place > 0))
    def _():
        @pl.when(jnp.logical_not(on_first))
        def _():
            row_copy(0, 0).start()

        for line in range(1, lines):
            row_copy(line, 0).start()
        lax.fori_loop(1, place, send_all, 0)

    @pl.when(early)
    def _():
        lax.fori_loop(skip_line, x, send_line, 0)

    @pl.when(first_one)
    def _():
        lax.fori_loop(1, lines, send_line, 0)
        lax.fori_loop(1, group, send_all, 0)

    @pl.when(late)
    def _():
        pl.semaphore_signal(ready, inc=1, device_id=other_half, device_id_type=MESH)
        for device, far in ((up, across_up), (down, across_down)):

            @pl.when(far)
            def _():
                pl.semaphore_signal(ready_edge, inc=1, device_id=device, device_id_type=MESH)

    def hello_line(line, carry):
        pl.semaphore_signal(
            hello, inc=1, device_id=(member(line, place), tile), device_id_type=MESH
        )
        return carry

    lax.fori_loop(skip_line, x, hello_line, 0)

    def halo_copy(side, s, far):
        where = my_part if far else pl.ds(0, cols)
        return pltpu.make_async_remote_copy(
            src_ref=own.at[s, edge_rows[side], where], dst_ref=halo.at[side, s, :, where],
            send_sem=halo_send.at[side, s], recv_sem=halo_recv.at[side, s],
            device_id=up if side == 0 else down, device_id_type=MESH,
        )

    def share_copy(side, s, step):
        return pltpu.make_async_remote_copy(
            src_ref=halo.at[side, s, :, my_part], dst_ref=halo.at[side, s, :, my_part],
            send_sem=share_send, recv_sem=share_recv.at[side, s, step - 1],
            device_id=(line_peer(step), tile), device_id_type=MESH,
        )

    def share_arrival(side, s, step):
        theirs = lax.rem(x + lines - step, lines)
        where = pl.ds(pl.multiple_of(theirs * part, part), part)
        return pltpu.make_async_remote_copy(
            src_ref=halo.at[side, s, :, where], dst_ref=halo.at[side, s, :, where],
            send_sem=share_send, recv_sem=share_recv.at[side, s, step - 1],
            device_id=(member(theirs, place), tile), device_id_type=MESH,
        )

    for copy in own_copies:
        copy.wait()
    for s in range(slices):
        for side, far in ((0, across_up), (1, across_down)):

            @pl.when(jnp.logical_and(late, far))
            def _():
                halo_copy(side, s, True).start()

            @pl.when(jnp.logical_not(far))
            def _():
                halo_copy(side, s, False).start()

    small_copies[2].wait()
    small_copies[3].wait()
    u, half = beam // 2, lax.rem(beam, 2)
    tiles = cols // 128
    extent = strip + 2 * HALO
    matrix0[...] = blur_matrix(0)
    matrix1[...] = blur_matrix(REACH)
    spread[0], spread[1] = spread_matrix()
    place_rows(ext, own, HALO, extent)

    @pl.when(jnp.logical_and(x < lines - 1, jnp.logical_not(first_one)))
    def _():
        pl.semaphore_wait(hello, lines - 1 - x)

    @pl.when(jnp.logical_and(early, jnp.logical_not(first_one)))
    def _():
        lax.fori_loop(x + 1, lines, send_line, 0)

    def collect(z, carry):
        for line in range(lines):
            row_arrival(line, z).wait_recv()
        return carry

    def answer(z, carry):
        for line in range(lines):
            row_arrival(line, z).wait_recv()
            row_copy(line, z).start()
        return carry

    answer_first = jnp.logical_or(across, place >= group // 2)

    @pl.when(jnp.logical_and(jnp.logical_and(early, answer_first), jnp.logical_not(first_one)))
    def _():
        lax.fori_loop(place + 1, group, answer, 0)

    for side, far in ((0, across_up), (1, across_down)):

        @pl.when(jnp.logical_and(early, far))
        def _():
            pl.semaphore_wait(ready_edge, 1)
            for s in range(slices):
                halo_copy(side, s, True).start()

    def collect_rows():
        @pl.when(jnp.logical_not(answer_first))
        def _():
            lax.fori_loop(place + 1, group, answer, 0)

        @pl.when(jnp.logical_and(on_first, place > 0))
        def _():
            row_arrival(0, 0).wait_recv()
            row_copy(0, 0).start()

        def collect_line(line, carry):
            row_arrival(line, place).wait_recv()
            return carry

        def collect_head(line, carry):
            row_arrival(line, 0).wait_recv()
            return carry

        lax.fori_loop(skip_line, x, collect_line, 0)
        lax.fori_loop(x + 1, lines, collect_line, 0)

        @pl.when(place > 0)
        def _():
            lax.fori_loop(skip_first, lines, collect_head, 0)

        lax.fori_loop(1, place, collect, 0)

        @pl.when(first_one)
        def _():
            lax.fori_loop(1, group, collect, 0)

        pl.semaphore_wait(ready, 1)
        table_copy.start()

    beside_first = jnp.logical_and(skip_line == 1, beam > 0)

    @pl.when(beside_first)
    def _():
        row_arrival(0, 0).wait_recv()
        row_copy(0, 0).start()

    for s in range(slices):
        for side, far in ((0, across_down), (1, across_up)):

            @pl.when(far)
            def _():
                halo_copy(side, s, True).wait_recv()
                for step in range(1, lines):
                    share_copy(side, s, step).start()


    @pl.when(jnp.logical_and(jnp.logical_and(early, across), jnp.logical_not(first_one)))
    def _():
        collect_rows()

    for s, (gathered, row, count, matrix, trans) in enumerate(
        ((first, 1, 32, matrix0, trans0), (second, 6, 24, matrix1, trans1))
    ):
        for side, far in ((0, across_down), (1, across_up)):

            @pl.when(far)
            def _():
                for step in range(1, lines):
                    share_arrival(side, s, step).wait_recv()

            @pl.when(jnp.logical_not(far))
            def _():
                halo_copy(side, s, False).wait_recv()

        place_halo(ext, halo, s, extent, strip)
        take_windows(ext, extent, tiles, probe_rows, probe_cols, gathered, s, row, count, u, half)
        transmission(gathered, blurred, matrix, trans)

    @pl.when(jnp.logical_or(first_one, jnp.logical_and(early, jnp.logical_not(across))))
    def _():
        collect_rows()

    @pl.when(late)
    def _():
        table_copy.wait_recv()

    wave[...] = probe_function(table[:, 0, :], u, half)
    result = propagate(wave, trans0, trans1, psi, both, spread, table.shape[0])
    turned = jnp.transpose(result)
    out[:, 0:32] = turned[0:8]
    out[:, 32:64] = turned[64:72]

    def sent(ref, semaphore):
        pltpu.make_async_remote_copy(
            src_ref=ref, dst_ref=ref, send_sem=semaphore, recv_sem=table_recv,
            device_id=other_half, device_id_type=MESH,
        ).wait_send()

    for s in range(slices):
        for side, far in ((0, across_up), (1, across_down)):

            @pl.when(far)
            def _():
                halo_copy(side, s, True).wait_send()

            @pl.when(jnp.logical_not(far))
            def _():
                halo_copy(side, s, False).wait_send()

    @pl.when(across)
    def _():
        sent(halo.at[0, :, :, pl.ds(0, (lines - 1) * part)], share_send)


    @pl.when(early)
    def _():
        table_copy.wait_send()

        sent(table.at[pl.ds(0, lines * group - 1)], row_send)


def body(atom_counts, beam_index, beam_weight, probe_rows, probe_cols):
    slices, strip, cols = atom_counts.shape
    beams = lax.axis_size("beam")
    lines = beams // 8
    hbm = pl.BlockSpec(memory_space=pltpu.HBM)
    dma = pltpu.SemaphoreType.DMA
    result = pl.pallas_call(
        kernel,
        out_shape=jax.ShapeDtypeStruct((8, probe_rows.shape[0]), F32),
        in_specs=[hbm] * 5,
        out_specs=pl.BlockSpec(memory_space=pltpu.VMEM),
        scratch_shapes=[
            pltpu.SMEM(probe_rows.shape, jnp.int32),
            pltpu.SMEM(probe_cols.shape, jnp.int32),
            pltpu.SMEM(beam_index.shape, jnp.int32),
            pltpu.SMEM(beam_weight.shape, F32),
            pltpu.VMEM((slices, strip, cols), BF16),
            pltpu.VMEM((2, slices, HALO, cols), BF16),
            pltpu.VMEM((beams, 1, 128), F32),
            pltpu.VMEM((slices * (strip + 2 * HALO) * cols // 128, 128), F32),
            pltpu.VMEM((32 * 32, 128), F32),
            pltpu.VMEM((24 * 32, 128), F32),
            pltpu.VMEM((32 * 32, 128), F32),
            pltpu.VMEM((128, 256), BF16),
            pltpu.VMEM((128, 256), BF16),
            pltpu.VMEM((2, 256, 256), BF16),
            pltpu.VMEM((2, 21 * 32, 128), F32),
            pltpu.VMEM((2, 11 * 32, 128), F32),
            pltpu.VMEM((128, 256), F32),
            pltpu.VMEM((2, 21 * 32, 128), F32),
            pltpu.VMEM((11 * 32, 256), F32),
            dma((2, slices)),
            dma((4,)),
            dma((2, slices)),
            dma((2, slices)),
            dma(()),
            dma((2, slices, lines - 1)),
            dma(()),
            dma((beams,)),
            dma(()),
            dma(()),
            pltpu.SemaphoreType.REGULAR,
            pltpu.SemaphoreType.REGULAR,
            pltpu.SemaphoreType.REGULAR,
        ],
        compiler_params=pltpu.CompilerParams(
            collective_id=0, has_side_effects=True, vmem_limit_bytes=64 * 2**20 - 2**18
        ),
    )(probe_rows, probe_cols, beam_index, beam_weight, atom_counts)
    return result.T


def solution(mesh):
    return jax.shard_map(
        body,
        mesh=mesh,
        in_specs=(P(None, "tile", None), P("beam", None), P("beam"), P("tile"), P("tile")),
        out_specs=P("tile", "beam"),
        check_vma=False,
    )
```

```python
import functools
import math

import jax
import jax.numpy as jnp
import numpy as np
from jax import lax
from jax.experimental import pallas as pl
from jax.experimental.pallas import tpu as pltpu
from jax.sharding import PartitionSpec as P

CROP = 16
REACH = 5
HALO = 16
CENTRE = 1.2
F32 = jnp.float32
BF16 = jnp.bfloat16
MESH = pl.DeviceIdType.MESH


def make_taps():
    offsets = np.arange(-REACH, REACH + 1, dtype=np.float64)
    blur = np.exp(-(offsets**2) / 4.5)
    blur = blur / blur.sum()
    weight = np.exp(-(offsets**2) / 18.0)
    weight = weight / weight.sum()
    spread = weight * np.exp(1j * 0.35 * offsets**2)
    return blur, spread


def fit(function, limit, terms):
    nodes = 0.5 * limit * (1.0 + np.cos(np.pi * (np.arange(64) + 0.5) / 64))
    return np.polynomial.Polynomial.fit(nodes, function(nodes), terms - 1, domain=[0, limit]).convert().coef


def horner(coefs, x):
    result = jnp.full_like(x, float(coefs[-1]))
    for coef in coefs[-2::-1]:
        result = result * x + float(coef)
    return result


def cos_sin_small(t):
    square = t * t
    root = np.sqrt
    even = fit(lambda s: np.cos(root(s)), 1.69, 6)
    odd = fit(lambda s: np.sin(root(s)) / root(s), 1.69, 5)
    return horner(even, square), t * horner(odd, square)


def cos_sin_turns(turns):
    turns = turns - jnp.floor(turns + 0.5)
    square = turns * turns
    full = lambda s: 2.0 * np.pi * np.sqrt(s)
    even = fit(lambda s: np.cos(full(s)), 0.25, 9)
    odd = fit(lambda s: np.sin(full(s)) / np.sqrt(s), 0.25, 8)
    return horner(even, square), turns * horner(odd, square)


def band(distance, values):
    result = jnp.zeros(distance.shape, F32)
    reach = jnp.abs(distance)
    for k in range(REACH + 1):
        result = jnp.where(reach == k, float(values[REACH + k]), result)
    return result


def split(x):
    high = x.astype(BF16)
    return high, (x - high.astype(F32)).astype(BF16)


def blur_matrix(shift):
    blur, _ = make_taps()
    rows = lax.broadcasted_iota(jnp.int32, (128, 128), 0)
    cols = lax.broadcasted_iota(jnp.int32, (128, 128), 1)
    values = band(rows - cols - shift - REACH, 0.6 * blur)
    high, low = split(jnp.where(rows // 64 == cols // 64, values, 0.0))
    return jnp.concatenate([high, low], axis=1)


def spread_matrix():
    _, spread = make_taps()
    turned = spread * np.exp(1j * CENTRE)
    rows = lax.broadcasted_iota(jnp.int32, (128, 128), 0)
    cols = lax.broadcasted_iota(jnp.int32, (128, 128), 1)
    same = rows // 64 == cols // 64
    distance = rows - cols - REACH
    real = jnp.where(same, band(distance, turned.real), 0.0)
    imag = jnp.where(same, band(distance, turned.imag), 0.0)
    whole = jnp.concatenate(
        [jnp.concatenate([real, imag], axis=1), jnp.concatenate([-imag, real], axis=1)], axis=0
    )
    return split(whole)


def dot(a, b):
    return jnp.dot(a, b, preferred_element_type=F32)


def dot3(x, high, low):
    x_high, x_low = split(x)
    return dot(x_high, high) + dot(x_low, high) + dot(x_high, low)


def place_rows(ext, source, first, extent):
    slices, rows, cols = source.shape
    tiles = cols // 128

    def one(tile, carry):
        for s in range(slices):
            block = source[s, :, pl.ds(pl.multiple_of(tile * 128, 128), 128)]
            start = pl.multiple_of((s * tiles + tile) * extent + first, 16)
            ext[pl.ds(start, rows), :] = block.astype(F32)
        return carry

    lax.fori_loop(0, tiles, one, 0, unroll=8)


def place_halo(ext, halo, s, extent, strip):
    tiles = halo.shape[3] // 128

    def one(tile, carry):
        for side, first in ((0, 0), (1, HALO + strip)):
            block = halo[side, s, :, pl.ds(pl.multiple_of(tile * 128, 128), 128)]
            start = pl.multiple_of((s * tiles + tile) * extent + first, 16)
            ext[pl.ds(start, HALO), :] = block.astype(F32)
        return carry

    lax.fori_loop(0, tiles, one, 0, unroll=8)


def take_windows(ext, extent, tiles, rows, cols, gathered, slice_index, first, count, u, half):
    cols_total = tiles * 128
    pairs = rows.shape[0] // 2
    lane = lax.broadcasted_iota(jnp.int32, (count, 128), 1)

    def window(probe, place):
        start = lax.rem(cols[probe] + (8 * half - 3 * REACH + cols_total), cols_total)
        tile, offset = start >> 7, start & 127
        after = lax.rem(tile + 1, tiles)
        row = rows[probe] + (u + first)
        near = ext[pl.ds((slice_index * tiles + tile) * extent + row, count), :]
        far = ext[pl.ds((slice_index * tiles + after) * extent + row, count), :]
        both = jnp.where(lane >= offset, near, far)
        return pltpu.roll(both, (128 - offset + place) & 127, 1)

    def one(pair, carry):
        joined = jnp.where(lane < 64, window(pair, 0), window(pair + pairs, 64))
        gathered[pl.ds(pair, count, stride=pairs), :] = joined
        return carry

    lax.fori_loop(0, pairs, one, 0, unroll=16)


def row_at(i, k):
    return pl.ds(pl.multiple_of((i + k) * 32, 32), 32)


def transmission(gathered, blurred, matrix, trans):
    blur, _ = make_taps()
    both = dot(gathered[...].astype(BF16), matrix[...])
    blurred[0 : gathered.shape[0], :] = both[:, :128] + both[:, 128:]

    def one(i, carry):
        total = float(blur[REACH]) * blurred[row_at(i, REACH), :] - CENTRE
        for k in range(REACH):
            near, far = blurred[row_at(i, k), :], blurred[row_at(i, 2 * REACH - k), :]
            total = total + float(blur[k]) * (near + far)
        trans[0, row_at(i, 0), :], trans[1, row_at(i, 0), :] = cos_sin_small(total)
        return carry

    rows = trans.shape[1] // 32
    lax.fori_loop(0, rows, one, 0, unroll=rows)


def spread_rows(psi, i):
    _, spread = make_taps()
    out_real, out_imag = None, None
    for k in range(REACH + 1):
        a, b = psi[0, row_at(i, k), :], psi[1, row_at(i, k), :]
        if k != REACH:
            a = a + psi[0, row_at(i, 2 * REACH - k), :]
            b = b + psi[1, row_at(i, 2 * REACH - k), :]
        c, s = float(spread[k].real), float(spread[k].imag)
        real, imag = c * a - s * b, c * b + s * a
        out_real = real if out_real is None else out_real + real
        out_imag = imag if out_imag is None else out_imag + imag
    return out_real, out_imag


def probe_function(table, u, half):
    kx, ky, weight = table[:, 0:1], table[:, 1:2], table[:, 2:3]
    lane = lax.broadcasted_iota(jnp.int32, (table.shape[0], 128), 1)
    down = (lane + (u - 2 * REACH)).astype(F32)
    across = (lax.rem(lane, 64) + (8 * half - 2 * REACH)).astype(F32)
    row_cos, row_sin = cos_sin_turns(kx * down * (1.0 / 512.0))
    col_cos, col_sin = cos_sin_turns(ky * across * (1.0 / 4096.0))
    left = jnp.concatenate([weight * row_cos, weight * row_sin], axis=0)
    right = jnp.concatenate(
        [
            jnp.concatenate([col_cos, col_sin], axis=1),
            jnp.concatenate([-col_sin, col_cos], axis=1),
        ],
        axis=0,
    )
    return lax.dot_general(
        left, right, (((0,), (0,)), ((), ())), precision=lax.Precision.HIGHEST,
        preferred_element_type=F32,
    )


def propagate(wave_ref, trans0, trans1, psi, both, spread, beams):
    rows0, rows1 = trans0.shape[1] // 32, trans1.shape[1] // 32

    def enter(i, carry):
        cos, sin = trans0[0, row_at(i, 0), :], trans0[1, row_at(i, 0), :]
        real = wave_ref[pl.ds(i, 1), 0:128]
        imag = wave_ref[pl.ds(i, 1), 128:256]
        psi[0, row_at(i, 0), :] = cos * real - sin * imag
        psi[1, row_at(i, 0), :] = cos * imag + sin * real
        return carry

    lax.fori_loop(0, rows0, enter, 0, unroll=rows0)

    def between(i, carry):
        both[row_at(i, 0), 0:128], both[row_at(i, 0), 128:256] = spread_rows(psi, i)
        return carry

    lax.fori_loop(0, rows1, between, 0, unroll=rows1)
    both[...] = dot3(both[...], spread[0], spread[1])

    def again(i, carry):
        real, imag = both[row_at(i, 0), 0:128], both[row_at(i, 0), 128:256]
        cos, sin = trans1[0, row_at(i, 0), :], trans1[1, row_at(i, 0), :]
        psi[0, row_at(i, 0), :] = real * cos - imag * sin
        psi[1, row_at(i, 0), :] = real * sin + imag * cos
        return carry

    lax.fori_loop(0, rows1, again, 0, unroll=rows1)
    last = dot3(jnp.concatenate(spread_rows(psi, 0), axis=1), spread[0], spread[1])
    return (last[:, :128] * last[:, :128] + last[:, 128:] * last[:, 128:]) * (1.0 / beams)


def kernel(
    rows_hbm, cols_hbm, index_hbm, weight_hbm, counts, out,
    probe_rows, probe_cols, beam_index, beam_weight,
    own, halo, table, ext, first, second, blurred, matrix0, matrix1, spread,
    trans0, trans1, wave, psi, both,
    own_sem, small_sem, halo_send, halo_recv, share_send, share_recv, row_send, row_recv,
    table_send, table_recv, ready, hello, ready_edge,
):
    beam, tile = lax.axis_index("beam"), lax.axis_index("tile")
    tiles_total = lax.axis_size("tile")
    group = 8
    lines = lax.axis_size("beam") // group
    half_tiles = tiles_total // 2
    x, place = beam // group, lax.rem(beam, group)
    early = tile < half_tiles
    late = jnp.logical_not(early)
    across_up = lax.rem(tile, half_tiles) == half_tiles - 1
    across_down = lax.rem(tile, half_tiles) == 0
    across = jnp.logical_or(across_up, across_down)
    mirrored = x * group + (group - 1 - place)
    up = (jnp.where(across_up, mirrored, beam), lax.rem(tile + 1, tiles_total))
    down = (jnp.where(across_down, mirrored, beam), lax.rem(tile + tiles_total - 1, tiles_total))
    other_half = (mirrored, lax.rem(tile + half_tiles, tiles_total))
    slices, strip, cols = own.shape
    part = cols // lines
    on_first = tile == 0
    first_one = jnp.logical_and(on_first, beam == 0)
    skip_first = on_first.astype(jnp.int32)
    skip_line = jnp.logical_and(on_first, place == 0).astype(jnp.int32)

    def member(line, z):
        return line * group + z

    def slot(line, z):
        return z * lines + line

    def line_peer(step):
        return member(lax.rem(x + step, lines), place)

    my_part = pl.ds(pl.multiple_of(x * part, part), part)
    edge_rows = (pl.ds(strip - HALO, HALO), pl.ds(0, HALO))
    own_copies = [
        pltpu.make_async_copy(
            counts.at[s, edge_rows[side]], own.at[s, edge_rows[side]], own_sem.at[side, s]
        )
        for s in range(slices)
        for side in (0, 1)
    ]
    for copy in own_copies:
        copy.start()
    small_copies = [
        pltpu.make_async_copy(source, target, small_sem.at[k])
        for k, (source, target) in enumerate(
            (
                (index_hbm, beam_index), (weight_hbm, beam_weight),
                (rows_hbm, probe_rows), (cols_hbm, probe_cols),
            )
        )
    ]
    for copy in small_copies:
        copy.start()

    barrier = pltpu.get_barrier_semaphore()

    def tell(device):
        pl.semaphore_signal(barrier, inc=1, device_id=device, device_id_type=MESH)

    @pl.when(jnp.logical_and(on_first, beam > 0))
    def _():
        tell((0, 0))

    for device, far in ((up, across_up), (down, across_down)):

        @pl.when(jnp.logical_or(early, jnp.logical_not(far)))
        def _():
            tell(device)

    def tell_line(line, carry):
        tell((member(line, place), tile))
        return carry

    def tell_later(z, carry):
        for line in range(lines):
            tell((member(line, z), tile))
        return carry

    @pl.when(jnp.logical_not(first_one))
    def _():
        lax.fori_loop(x + 1, lines, tell_line, 0)

    @pl.when(early)
    def _():
        tell(other_half)

        @pl.when(jnp.logical_not(first_one))
        def _():
            lax.fori_loop(place + 1, group, tell_later, 0)


    lane = lax.broadcasted_iota(jnp.int32, (1, 128), 1)
    small_copies[0].wait()
    small_copies[1].wait()

    @pl.when(early)
    def _():
        kx = beam_index[0, 0].astype(F32)
        ky = beam_index[0, 1].astype(F32)
        table[slot(x, place)] = jnp.where(
            lane == 0, kx, jnp.where(lane == 1, ky, jnp.where(lane == 2, beam_weight[0], 0.0))
        )

    across_count = across.astype(jnp.int32)
    expected = x + jnp.where(early, lines * place, 1 + across_count) - skip_first
    expected = jnp.where(first_one, lines * group - 1, expected) + 2 - across_count
    pl.semaphore_wait(barrier, expected)

    my_slot = slot(x, place)

    def row_copy(line, z):
        return pltpu.make_async_remote_copy(
            src_ref=table.at[my_slot], dst_ref=table.at[my_slot], send_sem=row_send,
            recv_sem=row_recv.at[my_slot], device_id=(member(line, z), tile), device_id_type=MESH,
        )

    def row_arrival(line, z):
        theirs = slot(line, z)
        return pltpu.make_async_remote_copy(
            src_ref=table.at[theirs], dst_ref=table.at[theirs], send_sem=row_send,
            recv_sem=row_recv.at[theirs], device_id=(member(line, z), tile), device_id_type=MESH,
        )

    table_copy = pltpu.make_async_remote_copy(
        src_ref=table, dst_ref=table, send_sem=table_send, recv_sem=table_recv,
        device_id=other_half, device_id_type=MESH,
    )

    def send_line(line, carry):
        row_copy(line, place).start()
        return carry

    def send_all(z, carry):
        for line in range(lines):
            row_copy(line, z).start()
        return carry

    @pl.when(jnp.logical_and(early, place > 0))
    def _():
        @pl.when(jnp.logical_not(on_first))
        def _():
            row_copy(0, 0).start()

        for line in range(1, lines):
            row_copy(line, 0).start()
        lax.fori_loop(1, place, send_all, 0)

    @pl.when(early)
    def _():
        lax.fori_loop(skip_line, x, send_line, 0)

    @pl.when(first_one)
    def _():
        lax.fori_loop(1, lines, send_line, 0)
        lax.fori_loop(1, group, send_all, 0)

    @pl.when(late)
    def _():
        pl.semaphore_signal(ready, inc=1, device_id=other_half, device_id_type=MESH)
        for device, far in ((up, across_up), (down, across_down)):

            @pl.when(far)
            def _():
                pl.semaphore_signal(ready_edge, inc=1, device_id=device, device_id_type=MESH)

    def hello_line(line, carry):
        pl.semaphore_signal(
            hello, inc=1, device_id=(member(line, place), tile), device_id_type=MESH
        )
        return carry

    lax.fori_loop(skip_line, x, hello_line, 0)

    def halo_copy(side, s, far):
        where = my_part if far else pl.ds(0, cols)
        return pltpu.make_async_remote_copy(
            src_ref=own.at[s, edge_rows[side], where], dst_ref=halo.at[side, s, :, where],
            send_sem=halo_send.at[side, s], recv_sem=halo_recv.at[side, s],
            device_id=up if side == 0 else down, device_id_type=MESH,
        )

    def share_copy(side, s, step):
        return pltpu.make_async_remote_copy(
            src_ref=halo.at[side, s, :, my_part], dst_ref=halo.at[side, s, :, my_part],
            send_sem=share_send, recv_sem=share_recv.at[side, s, step - 1],
            device_id=(line_peer(step), tile), device_id_type=MESH,
        )

    def share_arrival(side, s, step):
        theirs = lax.rem(x + lines - step, lines)
        where = pl.ds(pl.multiple_of(theirs * part, part), part)
        return pltpu.make_async_remote_copy(
            src_ref=halo.at[side, s, :, where], dst_ref=halo.at[side, s, :, where],
            send_sem=share_send, recv_sem=share_recv.at[side, s, step - 1],
            device_id=(member(theirs, place), tile), device_id_type=MESH,
        )

    for copy in own_copies:
        copy.wait()
    for s in range(slices):
        for side, far in ((0, across_up), (1, across_down)):

            @pl.when(jnp.logical_and(late, far))
            def _():
                halo_copy(side, s, True).start()

            @pl.when(jnp.logical_not(far))
            def _():
                halo_copy(side, s, False).start()

    small_copies[2].wait()
    small_copies[3].wait()
    u, half = beam // 2, lax.rem(beam, 2)
    tiles = cols // 128
    extent = strip + 2 * HALO
    matrix0[...] = blur_matrix(0)
    matrix1[...] = blur_matrix(REACH)
    spread[0], spread[1] = spread_matrix()
    place_rows(ext, own, HALO, extent)

    @pl.when(jnp.logical_and(x < lines - 1, jnp.logical_not(first_one)))
    def _():
        pl.semaphore_wait(hello, lines - 1 - x)

    @pl.when(jnp.logical_and(early, jnp.logical_not(first_one)))
    def _():
        lax.fori_loop(x + 1, lines, send_line, 0)

    def collect(z, carry):
        for line in range(lines):
            row_arrival(line, z).wait_recv()
        return carry

    def answer(z, carry):
        for line in range(lines):
            row_arrival(line, z).wait_recv()
            row_copy(line, z).start()
        return carry

    answer_first = jnp.logical_or(across, place >= group // 2)

    @pl.when(jnp.logical_and(jnp.logical_and(early, answer_first), jnp.logical_not(first_one)))
    def _():
        lax.fori_loop(place + 1, group, answer, 0)

    for side, far in ((0, across_up), (1, across_down)):

        @pl.when(jnp.logical_and(early, far))
        def _():
            pl.semaphore_wait(ready_edge, 1)
            for s in range(slices):
                halo_copy(side, s, True).start()

    def collect_rows():
        @pl.when(jnp.logical_not(answer_first))
        def _():
            lax.fori_loop(place + 1, group, answer, 0)

        @pl.when(jnp.logical_and(on_first, place > 0))
        def _():
            row_arrival(0, 0).wait_recv()
            row_copy(0, 0).start()

        def collect_line(line, carry):
            row_arrival(line, place).wait_recv()
            return carry

        def collect_head(line, carry):
            row_arrival(line, 0).wait_recv()
            return carry

        lax.fori_loop(skip_line, x, collect_line, 0)
        lax.fori_loop(x + 1, lines, collect_line, 0)

        @pl.when(place > 0)
        def _():
            lax.fori_loop(skip_first, lines, collect_head, 0)

        lax.fori_loop(1, place, collect, 0)

        @pl.when(first_one)
        def _():
            lax.fori_loop(1, group, collect, 0)

        pl.semaphore_wait(ready, 1)
        table_copy.start()

    beside_first = jnp.logical_and(skip_line == 1, beam > 0)

    @pl.when(beside_first)
    def _():
        row_arrival(0, 0).wait_recv()
        row_copy(0, 0).start()

    for s in range(slices):
        for side, far in ((0, across_down), (1, across_up)):

            @pl.when(far)
            def _():
                halo_copy(side, s, True).wait_recv()
                for step in range(1, lines):
                    share_copy(side, s, step).start()


    @pl.when(jnp.logical_and(jnp.logical_and(early, across), jnp.logical_not(first_one)))
    def _():
        collect_rows()

    for s, (gathered, row, count, matrix, trans) in enumerate(
        ((first, 1, 32, matrix0, trans0), (second, 6, 24, matrix1, trans1))
    ):
        for side, far in ((0, across_down), (1, across_up)):

            @pl.when(far)
            def _():
                for step in range(1, lines):
                    share_arrival(side, s, step).wait_recv()

            @pl.when(jnp.logical_not(far))
            def _():
                halo_copy(side, s, False).wait_recv()

        place_halo(ext, halo, s, extent, strip)
        take_windows(ext, extent, tiles, probe_rows, probe_cols, gathered, s, row, count, u, half)
        transmission(gathered, blurred, matrix, trans)

    @pl.when(jnp.logical_or(first_one, jnp.logical_and(early, jnp.logical_not(across))))
    def _():
        collect_rows()

    @pl.when(late)
    def _():
        table_copy.wait_recv()

    wave[...] = probe_function(table[:, 0, :], u, half)
    result = propagate(wave, trans0, trans1, psi, both, spread, table.shape[0])
    turned = jnp.transpose(result)
    out[:, 0:32] = turned[0:8]
    out[:, 32:64] = turned[64:72]

    def sent(ref, semaphore):
        pltpu.make_async_remote_copy(
            src_ref=ref, dst_ref=ref, send_sem=semaphore, recv_sem=table_recv,
            device_id=other_half, device_id_type=MESH,
        ).wait_send()

    for s in range(slices):
        for side, far in ((0, across_up), (1, across_down)):

            @pl.when(far)
            def _():
                halo_copy(side, s, True).wait_send()

            @pl.when(jnp.logical_not(far))
            def _():
                halo_copy(side, s, False).wait_send()

    @pl.when(across)
    def _():
        sent(halo.at[0, :, :, pl.ds(0, (lines - 1) * part)], share_send)


    @pl.when(early)
    def _():
        table_copy.wait_send()

        sent(table.at[pl.ds(0, lines * group - 1)], row_send)


def body(atom_counts, beam_index, beam_weight, probe_rows, probe_cols):
    slices, strip, cols = atom_counts.shape
    beams = lax.axis_size("beam")
    lines = beams // 8
    hbm = pl.BlockSpec(memory_space=pltpu.HBM)
    dma = pltpu.SemaphoreType.DMA
    result = pl.pallas_call(
        kernel,
        out_shape=pltpu.VMEM((8, probe_rows.shape[0]), F32),
        in_specs=[hbm] * 5,
        out_specs=pl.BlockSpec(memory_space=pltpu.VMEM),
        scratch_shapes=[
            pltpu.SMEM(probe_rows.shape, jnp.int32),
            pltpu.SMEM(probe_cols.shape, jnp.int32),
            pltpu.SMEM(beam_index.shape, jnp.int32),
            pltpu.SMEM(beam_weight.shape, F32),
            pltpu.VMEM((slices, strip, cols), BF16),
            pltpu.VMEM((2, slices, HALO, cols), BF16),
            pltpu.VMEM((beams, 1, 128), F32),
            pltpu.VMEM((slices * (strip + 2 * HALO) * cols // 128, 128), F32),
            pltpu.VMEM((32 * 32, 128), F32),
            pltpu.VMEM((24 * 32, 128), F32),
            pltpu.VMEM((32 * 32, 128), F32),
            pltpu.VMEM((128, 256), BF16),
            pltpu.VMEM((128, 256), BF16),
            pltpu.VMEM((2, 256, 256), BF16),
            pltpu.VMEM((2, 21 * 32, 128), F32),
            pltpu.VMEM((2, 11 * 32, 128), F32),
            pltpu.VMEM((128, 256), F32),
            pltpu.VMEM((2, 21 * 32, 128), F32),
            pltpu.VMEM((11 * 32, 256), F32),
            dma((2, slices)),
            dma((4,)),
            dma((2, slices)),
            dma((2, slices)),
            dma(()),
            dma((2, slices, lines - 1)),
            dma(()),
            dma((beams,)),
            dma(()),
            dma(()),
            pltpu.SemaphoreType.REGULAR,
            pltpu.SemaphoreType.REGULAR,
            pltpu.SemaphoreType.REGULAR,
        ],
        compiler_params=pltpu.CompilerParams(
            collective_id=0, has_side_effects=True, vmem_limit_bytes=64 * 2**20 - 2**18
        ),
    )(probe_rows, probe_cols, beam_index, beam_weight, atom_counts)
    return result.T


def solution(mesh):
    return jax.shard_map(
        body,
        mesh=mesh,
        in_specs=(P(None, "tile", None), P("beam", None), P("beam"), P("tile"), P("tile")),
        out_specs=P("tile", "beam"),
        check_vma=False,
    )
```

```python
import functools
import math

import jax
import jax.numpy as jnp
import numpy as np
from jax import lax
from jax.experimental import pallas as pl
from jax.experimental.pallas import tpu as pltpu
from jax.sharding import PartitionSpec as P

CROP = 16
REACH = 5
HALO = 16
CENTRE = 1.2
F32 = jnp.float32
BF16 = jnp.bfloat16
MESH = pl.DeviceIdType.MESH


def make_taps():
    offsets = np.arange(-REACH, REACH + 1, dtype=np.float64)
    blur = np.exp(-(offsets**2) / 4.5)
    blur = blur / blur.sum()
    weight = np.exp(-(offsets**2) / 18.0)
    weight = weight / weight.sum()
    spread = weight * np.exp(1j * 0.35 * offsets**2)
    return blur, spread


def fit(function, limit, terms):
    nodes = 0.5 * limit * (1.0 + np.cos(np.pi * (np.arange(64) + 0.5) / 64))
    return np.polynomial.Polynomial.fit(nodes, function(nodes), terms - 1, domain=[0, limit]).convert().coef


def horner(coefs, x):
    result = jnp.full_like(x, float(coefs[-1]))
    for coef in coefs[-2::-1]:
        result = result * x + float(coef)
    return result


def cos_sin_small(t):
    square = t * t
    root = np.sqrt
    even = fit(lambda s: np.cos(root(s)), 1.69, 6)
    odd = fit(lambda s: np.sin(root(s)) / root(s), 1.69, 5)
    return horner(even, square), t * horner(odd, square)


def cos_sin_turns(turns):
    turns = turns - jnp.floor(turns + 0.5)
    square = turns * turns
    full = lambda s: 2.0 * np.pi * np.sqrt(s)
    even = fit(lambda s: np.cos(full(s)), 0.25, 9)
    odd = fit(lambda s: np.sin(full(s)) / np.sqrt(s), 0.25, 8)
    return horner(even, square), turns * horner(odd, square)


def band(distance, values):
    result = jnp.zeros(distance.shape, F32)
    reach = jnp.abs(distance)
    for k in range(REACH + 1):
        result = jnp.where(reach == k, float(values[REACH + k]), result)
    return result


def split(x):
    high = x.astype(BF16)
    return high, (x - high.astype(F32)).astype(BF16)


def blur_matrix(shift):
    blur, _ = make_taps()
    rows = lax.broadcasted_iota(jnp.int32, (128, 128), 0)
    cols = lax.broadcasted_iota(jnp.int32, (128, 128), 1)
    values = band(rows - cols - shift - REACH, 0.6 * blur)
    high, low = split(jnp.where(rows // 64 == cols // 64, values, 0.0))
    return jnp.concatenate([high, low], axis=1)


def spread_matrix():
    _, spread = make_taps()
    turned = spread * np.exp(1j * CENTRE)
    rows = lax.broadcasted_iota(jnp.int32, (128, 128), 0)
    cols = lax.broadcasted_iota(jnp.int32, (128, 128), 1)
    same = rows // 64 == cols // 64
    distance = rows - cols - REACH
    real = jnp.where(same, band(distance, turned.real), 0.0)
    imag = jnp.where(same, band(distance, turned.imag), 0.0)
    whole = jnp.concatenate(
        [jnp.concatenate([real, imag], axis=1), jnp.concatenate([-imag, real], axis=1)], axis=0
    )
    return split(whole)


def dot(a, b):
    return jnp.dot(a, b, preferred_element_type=F32)


def dot3(x, high, low):
    x_high, x_low = split(x)
    return dot(x_high, high) + dot(x_low, high) + dot(x_high, low)


def place_rows(ext, source, first, extent):
    slices, rows, cols = source.shape
    tiles = cols // 128

    def one(tile, carry):
        for s in range(slices):
            block = source[s, :, pl.ds(pl.multiple_of(tile * 128, 128), 128)]
            start = pl.multiple_of((s * tiles + tile) * extent + first, 16)
            ext[pl.ds(start, rows), :] = block.astype(F32)
        return carry

    lax.fori_loop(0, tiles, one, 0, unroll=8)


def place_halo(ext, halo, s, extent, strip):
    tiles = halo.shape[3] // 128

    def one(tile, carry):
        for side, first in ((0, 0), (1, HALO + strip)):
            block = halo[side, s, :, pl.ds(pl.multiple_of(tile * 128, 128), 128)]
            start = pl.multiple_of((s * tiles + tile) * extent + first, 16)
            ext[pl.ds(start, HALO), :] = block.astype(F32)
        return carry

    lax.fori_loop(0, tiles, one, 0, unroll=8)


def take_windows(ext, extent, tiles, rows, cols, gathered, slice_index, first, count, u, half):
    cols_total = tiles * 128
    pairs = rows.shape[0] // 2
    lane = lax.broadcasted_iota(jnp.int32, (count, 128), 1)

    def window(probe, place):
        start = lax.rem(cols[probe] + (8 * half - 3 * REACH + cols_total), cols_total)
        tile, offset = start >> 7, start & 127
        after = lax.rem(tile + 1, tiles)
        row = rows[probe] + (u + first)
        near = ext[pl.ds((slice_index * tiles + tile) * extent + row, count), :]
        far = ext[pl.ds((slice_index * tiles + after) * extent + row, count), :]
        both = jnp.where(lane >= offset, near, far)
        return pltpu.roll(both, (128 - offset + place) & 127, 1)

    def one(pair, carry):
        joined = jnp.where(lane < 64, window(pair, 0), window(pair + pairs, 64))
        gathered[pl.ds(pair, count, stride=pairs), :] = joined
        return carry

    lax.fori_loop(0, pairs, one, 0, unroll=16)


def row_at(i, k):
    return pl.ds(pl.multiple_of((i + k) * 32, 32), 32)


def transmission(gathered, blurred, matrix, trans):
    blur, _ = make_taps()
    both = dot(gathered[...].astype(BF16), matrix[...])
    blurred[0 : gathered.shape[0], :] = both[:, :128] + both[:, 128:]

    def one(i, carry):
        total = float(blur[REACH]) * blurred[row_at(i, REACH), :] - CENTRE
        for k in range(REACH):
            near, far = blurred[row_at(i, k), :], blurred[row_at(i, 2 * REACH - k), :]
            total = total + float(blur[k]) * (near + far)
        trans[0, row_at(i, 0), :], trans[1, row_at(i, 0), :] = cos_sin_small(total)
        return carry

    rows = trans.shape[1] // 32
    lax.fori_loop(0, rows, one, 0, unroll=rows)


def spread_rows(psi, i):
    _, spread = make_taps()
    out_real, out_imag = None, None
    for k in range(REACH + 1):
        a, b = psi[0, row_at(i, k), :], psi[1, row_at(i, k), :]
        if k != REACH:
            a = a + psi[0, row_at(i, 2 * REACH - k), :]
            b = b + psi[1, row_at(i, 2 * REACH - k), :]
        c, s = float(spread[k].real), float(spread[k].imag)
        real, imag = c * a - s * b, c * b + s * a
        out_real = real if out_real is None else out_real + real
        out_imag = imag if out_imag is None else out_imag + imag
    return out_real, out_imag


def probe_function(table, u, half):
    kx, ky, weight = table[:, 0:1], table[:, 1:2], table[:, 2:3]
    lane = lax.broadcasted_iota(jnp.int32, (table.shape[0], 128), 1)
    down = (lane + (u - 2 * REACH)).astype(F32)
    across = (lax.rem(lane, 64) + (8 * half - 2 * REACH)).astype(F32)
    row_cos, row_sin = cos_sin_turns(kx * down * (1.0 / 512.0))
    col_cos, col_sin = cos_sin_turns(ky * across * (1.0 / 4096.0))
    left = jnp.concatenate([weight * row_cos, weight * row_sin], axis=0)
    right = jnp.concatenate(
        [
            jnp.concatenate([col_cos, col_sin], axis=1),
            jnp.concatenate([-col_sin, col_cos], axis=1),
        ],
        axis=0,
    )
    return lax.dot_general(
        left, right, (((0,), (0,)), ((), ())), precision=lax.Precision.HIGHEST,
        preferred_element_type=F32,
    )


def propagate(wave_ref, trans0, trans1, psi, both, spread, beams):
    rows0, rows1 = trans0.shape[1] // 32, trans1.shape[1] // 32

    def enter(i, carry):
        cos, sin = trans0[0, row_at(i, 0), :], trans0[1, row_at(i, 0), :]
        real = wave_ref[pl.ds(i, 1), 0:128]
        imag = wave_ref[pl.ds(i, 1), 128:256]
        psi[0, row_at(i, 0), :] = cos * real - sin * imag
        psi[1, row_at(i, 0), :] = cos * imag + sin * real
        return carry

    lax.fori_loop(0, rows0, enter, 0, unroll=rows0)

    def between(i, carry):
        both[row_at(i, 0), 0:128], both[row_at(i, 0), 128:256] = spread_rows(psi, i)
        return carry

    lax.fori_loop(0, rows1, between, 0, unroll=rows1)
    both[...] = dot3(both[...], spread[0], spread[1])

    def again(i, carry):
        real, imag = both[row_at(i, 0), 0:128], both[row_at(i, 0), 128:256]
        cos, sin = trans1[0, row_at(i, 0), :], trans1[1, row_at(i, 0), :]
        psi[0, row_at(i, 0), :] = real * cos - imag * sin
        psi[1, row_at(i, 0), :] = real * sin + imag * cos
        return carry

    lax.fori_loop(0, rows1, again, 0, unroll=rows1)
    last = dot3(jnp.concatenate(spread_rows(psi, 0), axis=1), spread[0], spread[1])
    return (last[:, :128] * last[:, :128] + last[:, 128:] * last[:, 128:]) * (1.0 / beams)


def kernel(
    rows_hbm, cols_hbm, index_hbm, weight_hbm, counts, out,
    probe_rows, probe_cols, beam_index, beam_weight,
    own, halo, table, whole, ext, first, second, blurred, matrix0, matrix1, spread,
    trans0, trans1, wave, psi, both,
    own_sem, small_sem, halo_send, halo_recv, share_send, share_recv, row_send, row_recv,
    table_send, table_recv, first_send, first_recv, ready, hello, ready_edge,
):
    beam, tile = lax.axis_index("beam"), lax.axis_index("tile")
    tiles_total = lax.axis_size("tile")
    group = 8
    lines = lax.axis_size("beam") // group
    half_tiles = tiles_total // 2
    x, place = beam // group, lax.rem(beam, group)
    early = tile < half_tiles
    late = jnp.logical_not(early)
    across_up = lax.rem(tile, half_tiles) == half_tiles - 1
    across_down = lax.rem(tile, half_tiles) == 0
    across = jnp.logical_or(across_up, across_down)
    mirrored = x * group + (group - 1 - place)
    up = (jnp.where(across_up, mirrored, beam), lax.rem(tile + 1, tiles_total))
    down = (jnp.where(across_down, mirrored, beam), lax.rem(tile + tiles_total - 1, tiles_total))
    other_half = (mirrored, lax.rem(tile + half_tiles, tiles_total))
    slices, strip, cols = own.shape
    part = cols // lines
    on_first = tile == 0
    first_one = jnp.logical_and(on_first, beam == 0)
    skip_first = on_first.astype(jnp.int32)
    skip_line = jnp.logical_and(on_first, place == 0).astype(jnp.int32)

    def member(line, z):
        return line * group + z

    def slot(line, z):
        return z * lines + line

    def line_peer(step):
        return member(lax.rem(x + step, lines), place)

    my_part = pl.ds(pl.multiple_of(x * part, part), part)
    edge_rows = (pl.ds(strip - HALO, HALO), pl.ds(0, HALO))
    own_copies = [
        pltpu.make_async_copy(
            counts.at[s, edge_rows[side]], own.at[s, edge_rows[side]], own_sem.at[side, s]
        )
        for s in range(slices)
        for side in (0, 1)
    ]
    for copy in own_copies:
        copy.start()
    small_copies = [
        pltpu.make_async_copy(source, target, small_sem.at[k])
        for k, (source, target) in enumerate(
            (
                (index_hbm, beam_index), (weight_hbm, beam_weight),
                (rows_hbm, probe_rows), (cols_hbm, probe_cols),
            )
        )
    ]
    for copy in small_copies:
        copy.start()

    whole[...] = jnp.zeros(whole.shape, F32)

    barrier = pltpu.get_barrier_semaphore()

    def tell(device):
        pl.semaphore_signal(barrier, inc=1, device_id=device, device_id_type=MESH)

    @pl.when(jnp.logical_and(on_first, beam > 0))
    def _():
        tell((0, 0))

    for device, far in ((up, across_up), (down, across_down)):

        @pl.when(jnp.logical_or(early, jnp.logical_not(far)))
        def _():
            tell(device)

    def tell_line(line, carry):
        tell((member(line, place), tile))
        return carry

    def tell_later(z, carry):
        for line in range(lines):
            tell((member(line, z), tile))
        return carry

    @pl.when(jnp.logical_not(first_one))
    def _():
        lax.fori_loop(x + 1, lines, tell_line, 0)

    @pl.when(early)
    def _():
        tell(other_half)

        @pl.when(jnp.logical_not(first_one))
        def _():
            lax.fori_loop(place + 1, group, tell_later, 0)


    lane = lax.broadcasted_iota(jnp.int32, (1, 128), 1)
    small_copies[0].wait()
    small_copies[1].wait()

    @pl.when(early)
    def _():
        kx = beam_index[0, 0].astype(F32)
        ky = beam_index[0, 1].astype(F32)
        table[slot(x, place)] = jnp.where(
            lane == 0, kx, jnp.where(lane == 1, ky, jnp.where(lane == 2, beam_weight[0], 0.0))
        )

    across_count = across.astype(jnp.int32)
    expected = x + jnp.where(early, lines * place, 1 + across_count) - skip_first
    expected = jnp.where(first_one, lines * group - 1, expected) + 2 - across_count
    pl.semaphore_wait(barrier, expected)

    my_slot = slot(x, place)

    def row_copy(line, z):
        return pltpu.make_async_remote_copy(
            src_ref=table.at[my_slot], dst_ref=table.at[my_slot], send_sem=row_send,
            recv_sem=row_recv.at[my_slot], device_id=(member(line, z), tile), device_id_type=MESH,
        )

    def row_arrival(line, z):
        theirs = slot(line, z)
        return pltpu.make_async_remote_copy(
            src_ref=table.at[theirs], dst_ref=table.at[theirs], send_sem=row_send,
            recv_sem=row_recv.at[theirs], device_id=(member(line, z), tile), device_id_type=MESH,
        )

    feeder = jnp.logical_and(on_first, beam == group)
    first_copy = pltpu.make_async_remote_copy(
        src_ref=table, dst_ref=whole, send_sem=first_send, recv_sem=first_recv,
        device_id=(0, 0), device_id_type=MESH,
    )
    first_table_copy = pltpu.make_async_remote_copy(
        src_ref=whole, dst_ref=table, send_sem=table_send, recv_sem=table_recv,
        device_id=other_half, device_id_type=MESH,
    )
    table_copy = pltpu.make_async_remote_copy(
        src_ref=table, dst_ref=table, send_sem=table_send, recv_sem=table_recv,
        device_id=other_half, device_id_type=MESH,
    )

    def send_line(line, carry):
        row_copy(line, place).start()
        return carry

    def send_all(z, carry):
        for line in range(lines):
            row_copy(line, z).start()
        return carry

    @pl.when(jnp.logical_and(early, place > 0))
    def _():
        @pl.when(jnp.logical_not(on_first))
        def _():
            row_copy(0, 0).start()

        for line in range(1, lines):
            row_copy(line, 0).start()
        lax.fori_loop(1, place, send_all, 0)

    @pl.when(early)
    def _():
        lax.fori_loop(skip_line, x, send_line, 0)

    @pl.when(first_one)
    def _():
        lax.fori_loop(1, lines, send_line, 0)
        lax.fori_loop(1, group, send_all, 0)

    @pl.when(late)
    def _():
        pl.semaphore_signal(ready, inc=1, device_id=other_half, device_id_type=MESH)
        for device, far in ((up, across_up), (down, across_down)):

            @pl.when(far)
            def _():
                pl.semaphore_signal(ready_edge, inc=1, device_id=device, device_id_type=MESH)

    def hello_line(line, carry):
        pl.semaphore_signal(
            hello, inc=1, device_id=(member(line, place), tile), device_id_type=MESH
        )
        return carry

    lax.fori_loop(skip_line, x, hello_line, 0)

    def halo_copy(side, s, far):
        where = my_part if far else pl.ds(0, cols)
        return pltpu.make_async_remote_copy(
            src_ref=own.at[s, edge_rows[side], where], dst_ref=halo.at[side, s, :, where],
            send_sem=halo_send.at[side, s], recv_sem=halo_recv.at[side, s],
            device_id=up if side == 0 else down, device_id_type=MESH,
        )

    def share_copy(side, s, step):
        return pltpu.make_async_remote_copy(
            src_ref=halo.at[side, s, :, my_part], dst_ref=halo.at[side, s, :, my_part],
            send_sem=share_send, recv_sem=share_recv.at[side, s, step - 1],
            device_id=(line_peer(step), tile), device_id_type=MESH,
        )

    def share_arrival(side, s, step):
        theirs = lax.rem(x + lines - step, lines)
        where = pl.ds(pl.multiple_of(theirs * part, part), part)
        return pltpu.make_async_remote_copy(
            src_ref=halo.at[side, s, :, where], dst_ref=halo.at[side, s, :, where],
            send_sem=share_send, recv_sem=share_recv.at[side, s, step - 1],
            device_id=(member(theirs, place), tile), device_id_type=MESH,
        )

    for copy in own_copies:
        copy.wait()
    for s in range(slices):
        for side, far in ((0, across_up), (1, across_down)):

            @pl.when(jnp.logical_and(late, far))
            def _():
                halo_copy(side, s, True).start()

            @pl.when(jnp.logical_not(far))
            def _():
                halo_copy(side, s, False).start()

    small_copies[2].wait()
    small_copies[3].wait()
    u, half = beam // 2, lax.rem(beam, 2)
    tiles = cols // 128
    extent = strip + 2 * HALO
    matrix0[...] = blur_matrix(0)
    matrix1[...] = blur_matrix(REACH)
    spread[0], spread[1] = spread_matrix()
    place_rows(ext, own, HALO, extent)

    @pl.when(jnp.logical_and(x < lines - 1, jnp.logical_not(first_one)))
    def _():
        pl.semaphore_wait(hello, lines - 1 - x)

    @pl.when(jnp.logical_and(early, jnp.logical_not(first_one)))
    def _():
        lax.fori_loop(x + 1, lines, send_line, 0)

    def collect(z, carry):
        for line in range(lines):
            row_arrival(line, z).wait_recv()
        return carry

    def answer(z, carry):
        for line in range(lines):
            row_arrival(line, z).wait_recv()
            row_copy(line, z).start()
        return carry

    for side, far in ((0, across_up), (1, across_down)):

        @pl.when(jnp.logical_and(early, far))
        def _():
            pl.semaphore_wait(ready_edge, 1)
            for s in range(slices):
                halo_copy(side, s, True).start()

    answer_first = jnp.logical_or(across, place >= group // 2)

    @pl.when(jnp.logical_and(jnp.logical_and(early, answer_first), jnp.logical_not(first_one)))
    def _():
        lax.fori_loop(place + 1, group, answer, 0)

    def collect_rows():
        @pl.when(jnp.logical_not(answer_first))
        def _():
            lax.fori_loop(place + 1, group, answer, 0)

        @pl.when(jnp.logical_and(on_first, place > 0))
        def _():
            row_arrival(0, 0).wait_recv()

        def collect_line(line, carry):
            row_arrival(line, place).wait_recv()
            return carry

        def collect_head(line, carry):
            row_arrival(line, 0).wait_recv()
            return carry

        lax.fori_loop(skip_line, x, collect_line, 0)

        @pl.when(jnp.logical_not(first_one))
        def _():
            lax.fori_loop(x + 1, lines, collect_line, 0)

        @pl.when(place > 0)
        def _():
            lax.fori_loop(skip_first, lines, collect_head, 0)

        lax.fori_loop(1, place, collect, 0)

        @pl.when(first_one)
        def _():
            first_copy.wait_recv()

        @pl.when(feeder)
        def _():
            first_copy.start()

        pl.semaphore_wait(ready, 1)

        @pl.when(first_one)
        def _():
            first_table_copy.start()

        @pl.when(jnp.logical_not(first_one))
        def _():
            table_copy.start()


    beside_first = jnp.logical_and(skip_line == 1, beam > 0)

    @pl.when(beside_first)
    def _():
        row_arrival(0, 0).wait_recv()

    for s in range(slices):
        for side, far in ((0, across_down), (1, across_up)):

            @pl.when(far)
            def _():
                halo_copy(side, s, True).wait_recv()
                for step in range(1, lines):
                    share_copy(side, s, step).start()


    @pl.when(jnp.logical_and(jnp.logical_and(early, across), jnp.logical_not(first_one)))
    def _():
        collect_rows()

    for s, (gathered, row, count, matrix, trans) in enumerate(
        ((first, 1, 32, matrix0, trans0), (second, 6, 24, matrix1, trans1))
    ):
        for side, far in ((0, across_down), (1, across_up)):

            @pl.when(far)
            def _():
                for step in range(1, lines):
                    share_arrival(side, s, step).wait_recv()

            @pl.when(jnp.logical_not(far))
            def _():
                halo_copy(side, s, False).wait_recv()

        place_halo(ext, halo, s, extent, strip)
        take_windows(ext, extent, tiles, probe_rows, probe_cols, gathered, s, row, count, u, half)
        transmission(gathered, blurred, matrix, trans)

    @pl.when(jnp.logical_or(first_one, jnp.logical_and(early, jnp.logical_not(across))))
    def _():
        collect_rows()

    @pl.when(late)
    def _():
        table_copy.wait_recv()

    rows = jnp.where(first_one, whole[:, 0, :], table[:, 0, :])
    wave[...] = probe_function(rows, u, half)
    result = propagate(wave, trans0, trans1, psi, both, spread, table.shape[0])
    turned = jnp.transpose(result)
    out[:, 0:32] = turned[0:8]
    out[:, 32:64] = turned[64:72]

    def sent(ref, semaphore):
        pltpu.make_async_remote_copy(
            src_ref=ref, dst_ref=ref, send_sem=semaphore, recv_sem=table_recv,
            device_id=other_half, device_id_type=MESH,
        ).wait_send()

    for s in range(slices):
        for side, far in ((0, across_up), (1, across_down)):

            @pl.when(far)
            def _():
                halo_copy(side, s, True).wait_send()

            @pl.when(jnp.logical_not(far))
            def _():
                halo_copy(side, s, False).wait_send()

    @pl.when(across)
    def _():
        sent(halo.at[0, :, :, pl.ds(0, (lines - 1) * part)], share_send)


    @pl.when(early)
    def _():
        table_copy.wait_send()


        @pl.when(jnp.logical_and(on_first, beam > 0))
        def _():
            sent(table.at[pl.ds(0, lines * group - 2)], row_send)

        @pl.when(jnp.logical_not(jnp.logical_and(on_first, beam > 0)))
        def _():
            sent(table.at[pl.ds(0, lines * group - 1)], row_send)

    @pl.when(feeder)
    def _():
        first_copy.wait_send()


def body(atom_counts, beam_index, beam_weight, probe_rows, probe_cols):
    slices, strip, cols = atom_counts.shape
    beams = lax.axis_size("beam")
    lines = beams // 8
    hbm = pl.BlockSpec(memory_space=pltpu.HBM)
    dma = pltpu.SemaphoreType.DMA
    result = pl.pallas_call(
        kernel,
        out_shape=pltpu.VMEM((8, probe_rows.shape[0]), F32),
        in_specs=[hbm] * 5,
        out_specs=pl.BlockSpec(memory_space=pltpu.VMEM),
        scratch_shapes=[
            pltpu.SMEM(probe_rows.shape, jnp.int32),
            pltpu.SMEM(probe_cols.shape, jnp.int32),
            pltpu.SMEM(beam_index.shape, jnp.int32),
            pltpu.SMEM(beam_weight.shape, F32),
            pltpu.VMEM((slices, strip, cols), BF16),
            pltpu.VMEM((2, slices, HALO, cols), BF16),
            pltpu.VMEM((beams, 1, 128), F32),
            pltpu.VMEM((beams, 1, 128), F32),
            pltpu.VMEM((slices * (strip + 2 * HALO) * cols // 128, 128), F32),
            pltpu.VMEM((32 * 32, 128), F32),
            pltpu.VMEM((24 * 32, 128), F32),
            pltpu.VMEM((32 * 32, 128), F32),
            pltpu.VMEM((128, 256), BF16),
            pltpu.VMEM((128, 256), BF16),
            pltpu.VMEM((2, 256, 256), BF16),
            pltpu.VMEM((2, 21 * 32, 128), F32),
            pltpu.VMEM((2, 11 * 32, 128), F32),
            pltpu.VMEM((128, 256), F32),
            pltpu.VMEM((2, 21 * 32, 128), F32),
            pltpu.VMEM((11 * 32, 256), F32),
            dma((2, slices)),
            dma((4,)),
            dma((2, slices)),
            dma((2, slices)),
            dma(()),
            dma((2, slices, lines - 1)),
            dma(()),
            dma((beams,)),
            dma(()),
            dma(()),
            dma(()),
            dma(()),
            pltpu.SemaphoreType.REGULAR,
            pltpu.SemaphoreType.REGULAR,
            pltpu.SemaphoreType.REGULAR,
        ],
        compiler_params=pltpu.CompilerParams(
            collective_id=0, has_side_effects=True, vmem_limit_bytes=64 * 2**20 - 2**18
        ),
    )(probe_rows, probe_cols, beam_index, beam_weight, atom_counts)
    return result.T


def solution(mesh):
    return jax.shard_map(
        body,
        mesh=mesh,
        in_specs=(P(None, "tile", None), P("beam", None), P("beam"), P("tile"), P("tile")),
        out_specs=P("tile", "beam"),
        check_vma=False,
    )
```

```python
import functools
import math

import jax
import jax.numpy as jnp
import numpy as np
from jax import lax
from jax.experimental import pallas as pl
from jax.experimental.pallas import tpu as pltpu
from jax.sharding import PartitionSpec as P

CROP = 16
REACH = 5
HALO = 16
CENTRE = 1.2
F32 = jnp.float32
BF16 = jnp.bfloat16
MESH = pl.DeviceIdType.MESH


def make_taps():
    offsets = np.arange(-REACH, REACH + 1, dtype=np.float64)
    blur = np.exp(-(offsets**2) / 4.5)
    blur = blur / blur.sum()
    weight = np.exp(-(offsets**2) / 18.0)
    weight = weight / weight.sum()
    spread = weight * np.exp(1j * 0.35 * offsets**2)
    return blur, spread


def fit(function, limit, terms):
    nodes = 0.5 * limit * (1.0 + np.cos(np.pi * (np.arange(64) + 0.5) / 64))
    return np.polynomial.Polynomial.fit(nodes, function(nodes), terms - 1, domain=[0, limit]).convert().coef


def horner(coefs, x):
    result = jnp.full_like(x, float(coefs[-1]))
    for coef in coefs[-2::-1]:
        result = result * x + float(coef)
    return result


def cos_sin_small(t):
    square = t * t
    root = np.sqrt
    even = fit(lambda s: np.cos(root(s)), 1.69, 6)
    odd = fit(lambda s: np.sin(root(s)) / root(s), 1.69, 5)
    return horner(even, square), t * horner(odd, square)


def cos_sin_turns(turns):
    turns = turns - jnp.floor(turns + 0.5)
    square = turns * turns
    full = lambda s: 2.0 * np.pi * np.sqrt(s)
    even = fit(lambda s: np.cos(full(s)), 0.25, 9)
    odd = fit(lambda s: np.sin(full(s)) / np.sqrt(s), 0.25, 8)
    return horner(even, square), turns * horner(odd, square)


def band(distance, values):
    result = jnp.zeros(distance.shape, F32)
    reach = jnp.abs(distance)
    for k in range(REACH + 1):
        result = jnp.where(reach == k, float(values[REACH + k]), result)
    return result


def split(x):
    high = x.astype(BF16)
    return high, (x - high.astype(F32)).astype(BF16)


def blur_matrix(shift):
    blur, _ = make_taps()
    rows = lax.broadcasted_iota(jnp.int32, (128, 128), 0)
    cols = lax.broadcasted_iota(jnp.int32, (128, 128), 1)
    values = band(rows - cols - shift - REACH, 0.6 * blur)
    high, low = split(jnp.where(rows // 64 == cols // 64, values, 0.0))
    return jnp.concatenate([high, low], axis=1)


def spread_matrix():
    _, spread = make_taps()
    turned = spread * np.exp(1j * CENTRE)
    rows = lax.broadcasted_iota(jnp.int32, (128, 128), 0)
    cols = lax.broadcasted_iota(jnp.int32, (128, 128), 1)
    same = rows // 64 == cols // 64
    distance = rows - cols - REACH
    real = jnp.where(same, band(distance, turned.real), 0.0)
    imag = jnp.where(same, band(distance, turned.imag), 0.0)
    whole = jnp.concatenate(
        [jnp.concatenate([real, imag], axis=1), jnp.concatenate([-imag, real], axis=1)], axis=0
    )
    return split(whole)


def dot(a, b):
    return jnp.dot(a, b, preferred_element_type=F32)


def dot3(x, high, low):
    x_high, x_low = split(x)
    return dot(x_high, high) + dot(x_low, high) + dot(x_high, low)


def place_rows(ext, source, first, extent):
    slices, rows, cols = source.shape
    tiles = cols // 128

    def one(tile, carry):
        for s in range(slices):
            block = source[s, :, pl.ds(pl.multiple_of(tile * 128, 128), 128)]
            start = pl.multiple_of((s * tiles + tile) * extent + first, 16)
            ext[pl.ds(start, rows), :] = block.astype(F32)
        return carry

    lax.fori_loop(0, tiles, one, 0, unroll=8)


def place_halo(ext, halo, side, s, extent, strip):
    tiles = halo.shape[3] // 128

    def one(tile, carry):
        block = halo[side, s, :, pl.ds(pl.multiple_of(tile * 128, 128), 128)]
        start = pl.multiple_of((s * tiles + tile) * extent + side * (HALO + strip), 16)
        ext[pl.ds(start, HALO), :] = block.astype(F32)
        return carry

    lax.fori_loop(0, tiles, one, 0, unroll=8)


def clear_halo(ext, side, s, tiles, extent, strip):
    def one(tile, carry):
        start = pl.multiple_of((s * tiles + tile) * extent + side * (HALO + strip), 16)
        ext[pl.ds(start, HALO), :] = jnp.zeros((HALO, 128), F32)
        return carry

    lax.fori_loop(0, tiles, one, 0, unroll=8)


def take_windows(
    ext, extent, tiles, rows, cols, gathered, slice_index, first, count, u, half, base=0
):
    cols_total = tiles * 128
    pairs = rows.shape[0] // 2
    lane = lax.broadcasted_iota(jnp.int32, (count, 128), 1)

    def window(probe, place):
        start = lax.rem(cols[probe] + (8 * half - 3 * REACH + cols_total), cols_total)
        tile, offset = start >> 7, start & 127
        after = lax.rem(tile + 1, tiles)
        row = rows[probe] + (u + first + base)
        near = ext[pl.ds((slice_index * tiles + tile) * extent + row, count), :]
        far = ext[pl.ds((slice_index * tiles + after) * extent + row, count), :]
        both = jnp.where(lane >= offset, near, far)
        return pltpu.roll(both, (128 - offset + place) & 127, 1)

    def one(pair, carry):
        joined = jnp.where(lane < 64, window(pair, 0), window(pair + pairs, 64))
        gathered[pl.ds(base * pairs + pair, count, stride=pairs), :] = joined
        return carry

    lax.fori_loop(0, pairs, one, 0, unroll=8)


def row_at(i, k):
    return pl.ds(pl.multiple_of((i + k) * 32, 32), 32)


def transmission(gathered, blurred, matrix, trans):
    blur, _ = make_taps()
    both = dot(gathered[...].astype(BF16), matrix[...])
    blurred[0 : gathered.shape[0], :] = both[:, :128] + both[:, 128:]

    def one(i, carry):
        total = float(blur[REACH]) * blurred[row_at(i, REACH), :] - CENTRE
        for k in range(REACH):
            near, far = blurred[row_at(i, k), :], blurred[row_at(i, 2 * REACH - k), :]
            total = total + float(blur[k]) * (near + far)
        trans[0, row_at(i, 0), :], trans[1, row_at(i, 0), :] = cos_sin_small(total)
        return carry

    rows = trans.shape[1] // 32
    lax.fori_loop(0, rows, one, 0, unroll=rows)


def spread_rows(psi, i):
    _, spread = make_taps()
    out_real, out_imag = None, None
    for k in range(REACH + 1):
        a, b = psi[0, row_at(i, k), :], psi[1, row_at(i, k), :]
        if k != REACH:
            a = a + psi[0, row_at(i, 2 * REACH - k), :]
            b = b + psi[1, row_at(i, 2 * REACH - k), :]
        c, s = float(spread[k].real), float(spread[k].imag)
        real, imag = c * a - s * b, c * b + s * a
        out_real = real if out_real is None else out_real + real
        out_imag = imag if out_imag is None else out_imag + imag
    return out_real, out_imag


def probe_function(table, u, half):
    kx, ky, weight = table[:, 0:1], table[:, 1:2], table[:, 2:3]
    lane = lax.broadcasted_iota(jnp.int32, (table.shape[0], 128), 1)
    down = (lane + (u - 2 * REACH)).astype(F32)
    across = (lax.rem(lane, 64) + (8 * half - 2 * REACH)).astype(F32)
    row_cos, row_sin = cos_sin_turns(kx * down * (1.0 / 512.0))
    col_cos, col_sin = cos_sin_turns(ky * across * (1.0 / 4096.0))
    left = jnp.concatenate([weight * row_cos, weight * row_sin], axis=0)
    right = jnp.concatenate(
        [
            jnp.concatenate([col_cos, col_sin], axis=1),
            jnp.concatenate([-col_sin, col_cos], axis=1),
        ],
        axis=0,
    )
    return lax.dot_general(
        left, right, (((0,), (0,)), ((), ())), precision=lax.Precision.HIGHEST,
        preferred_element_type=F32,
    )


def propagate(wave_ref, trans0, trans1, psi, both, spread, beams):
    rows0, rows1 = trans0.shape[1] // 32, trans1.shape[1] // 32

    def enter(i, carry):
        cos, sin = trans0[0, row_at(i, 0), :], trans0[1, row_at(i, 0), :]
        real = wave_ref[pl.ds(i, 1), 0:128]
        imag = wave_ref[pl.ds(i, 1), 128:256]
        psi[0, row_at(i, 0), :] = cos * real - sin * imag
        psi[1, row_at(i, 0), :] = cos * imag + sin * real
        return carry

    lax.fori_loop(0, rows0, enter, 0, unroll=rows0)

    def between(i, carry):
        both[row_at(i, 0), 0:128], both[row_at(i, 0), 128:256] = spread_rows(psi, i)
        return carry

    lax.fori_loop(0, rows1, between, 0, unroll=rows1)
    both[...] = dot3(both[...], spread[0], spread[1])

    def again(i, carry):
        real, imag = both[row_at(i, 0), 0:128], both[row_at(i, 0), 128:256]
        cos, sin = trans1[0, row_at(i, 0), :], trans1[1, row_at(i, 0), :]
        psi[0, row_at(i, 0), :] = real * cos - imag * sin
        psi[1, row_at(i, 0), :] = real * sin + imag * cos
        return carry

    lax.fori_loop(0, rows1, again, 0, unroll=rows1)
    last = dot3(jnp.concatenate(spread_rows(psi, 0), axis=1), spread[0], spread[1])
    return (last[:, :128] * last[:, :128] + last[:, 128:] * last[:, 128:]) * (1.0 / beams)


def kernel(
    rows_hbm, cols_hbm, index_hbm, weight_hbm, counts, out,
    probe_rows, probe_cols, beam_index, beam_weight,
    own, halo, table, whole, ext, first, second, blurred, matrix0, matrix1, spread,
    trans0, trans1, wave, psi, both,
    own_sem, small_sem, halo_send, halo_recv, share_send, share_recv, row_send, row_recv,
    table_send, table_recv, first_send, first_recv, ready, hello, ready_edge,
):
    beam, tile = lax.axis_index("beam"), lax.axis_index("tile")
    tiles_total = lax.axis_size("tile")
    group = 8
    lines = lax.axis_size("beam") // group
    half_tiles = tiles_total // 2
    x, place = beam // group, lax.rem(beam, group)
    early = tile < half_tiles
    late = jnp.logical_not(early)
    across_up = lax.rem(tile, half_tiles) == half_tiles - 1
    across_down = lax.rem(tile, half_tiles) == 0
    across = jnp.logical_or(across_up, across_down)
    mirrored = x * group + (group - 1 - place)
    up = (jnp.where(across_up, mirrored, beam), lax.rem(tile + 1, tiles_total))
    down = (jnp.where(across_down, mirrored, beam), lax.rem(tile + tiles_total - 1, tiles_total))
    other_half = (mirrored, lax.rem(tile + half_tiles, tiles_total))
    slices, strip, cols = own.shape
    part = cols // lines
    on_first = tile == 0
    first_one = jnp.logical_and(on_first, beam == 0)
    skip_first = on_first.astype(jnp.int32)
    skip_line = jnp.logical_and(on_first, place == 0).astype(jnp.int32)

    def member(line, z):
        return line * group + z

    def slot(line, z):
        return z * lines + line

    def line_peer(step):
        return member(lax.rem(x + step, lines), place)

    my_part = pl.ds(pl.multiple_of(x * part, part), part)
    edge_rows = (pl.ds(strip - HALO, HALO), pl.ds(0, HALO))
    own_copies = [
        pltpu.make_async_copy(
            counts.at[s, edge_rows[side]], own.at[s, edge_rows[side]], own_sem.at[side, s]
        )
        for s in range(slices)
        for side in (0, 1)
    ]
    for copy in own_copies:
        copy.start()
    small_copies = [
        pltpu.make_async_copy(source, target, small_sem.at[k])
        for k, (source, target) in enumerate(
            (
                (index_hbm, beam_index), (weight_hbm, beam_weight),
                (rows_hbm, probe_rows), (cols_hbm, probe_cols),
            )
        )
    ]
    for copy in small_copies:
        copy.start()

    whole[...] = jnp.zeros(whole.shape, F32)

    barrier = pltpu.get_barrier_semaphore()

    def tell(device):
        pl.semaphore_signal(barrier, inc=1, device_id=device, device_id_type=MESH)

    @pl.when(jnp.logical_and(on_first, beam > 0))
    def _():
        tell((0, 0))

    for device, far in ((up, across_up), (down, across_down)):

        @pl.when(jnp.logical_or(early, jnp.logical_not(far)))
        def _():
            tell(device)

    def tell_line(line, carry):
        tell((member(line, place), tile))
        return carry

    def tell_later(z, carry):
        for line in range(lines):
            tell((member(line, z), tile))
        return carry

    @pl.when(jnp.logical_not(first_one))
    def _():
        lax.fori_loop(x + 1, lines, tell_line, 0)

    @pl.when(early)
    def _():
        tell(other_half)

        @pl.when(jnp.logical_not(first_one))
        def _():
            lax.fori_loop(place + 1, group, tell_later, 0)


    lane = lax.broadcasted_iota(jnp.int32, (1, 128), 1)
    small_copies[0].wait()
    small_copies[1].wait()

    @pl.when(early)
    def _():
        kx = beam_index[0, 0].astype(F32)
        ky = beam_index[0, 1].astype(F32)
        table[slot(x, place)] = jnp.where(
            lane == 0, kx, jnp.where(lane == 1, ky, jnp.where(lane == 2, beam_weight[0], 0.0))
        )

    across_count = across.astype(jnp.int32)
    expected = x + jnp.where(early, lines * place, 1 + across_count) - skip_first
    expected = jnp.where(first_one, lines * group - 1, expected) + 2 - across_count
    pl.semaphore_wait(barrier, expected)

    my_slot = slot(x, place)

    def row_copy(line, z):
        return pltpu.make_async_remote_copy(
            src_ref=table.at[my_slot], dst_ref=table.at[my_slot], send_sem=row_send,
            recv_sem=row_recv.at[my_slot], device_id=(member(line, z), tile), device_id_type=MESH,
        )

    def row_arrival(line, z):
        theirs = slot(line, z)
        return pltpu.make_async_remote_copy(
            src_ref=table.at[theirs], dst_ref=table.at[theirs], send_sem=row_send,
            recv_sem=row_recv.at[theirs], device_id=(member(line, z), tile), device_id_type=MESH,
        )

    feeder = jnp.logical_and(on_first, beam == group)
    first_copy = pltpu.make_async_remote_copy(
        src_ref=table, dst_ref=whole, send_sem=first_send, recv_sem=first_recv,
        device_id=(0, 0), device_id_type=MESH,
    )
    first_table_copy = pltpu.make_async_remote_copy(
        src_ref=whole, dst_ref=table, send_sem=table_send, recv_sem=table_recv,
        device_id=other_half, device_id_type=MESH,
    )
    table_copy = pltpu.make_async_remote_copy(
        src_ref=table, dst_ref=table, send_sem=table_send, recv_sem=table_recv,
        device_id=other_half, device_id_type=MESH,
    )

    def send_line(line, carry):
        row_copy(line, place).start()
        return carry

    def send_all(z, carry):
        for line in range(lines):
            row_copy(line, z).start()
        return carry

    @pl.when(jnp.logical_and(early, place > 0))
    def _():
        @pl.when(jnp.logical_not(on_first))
        def _():
            row_copy(0, 0).start()

        for line in range(1, lines):
            row_copy(line, 0).start()
        lax.fori_loop(1, place, send_all, 0)

    @pl.when(early)
    def _():
        lax.fori_loop(skip_line, x, send_line, 0)

    @pl.when(first_one)
    def _():
        lax.fori_loop(1, lines, send_line, 0)
        lax.fori_loop(1, group, send_all, 0)

    @pl.when(late)
    def _():
        pl.semaphore_signal(ready, inc=1, device_id=other_half, device_id_type=MESH)
        for device, far in ((up, across_up), (down, across_down)):

            @pl.when(far)
            def _():
                pl.semaphore_signal(ready_edge, inc=1, device_id=device, device_id_type=MESH)

    def hello_line(line, carry):
        pl.semaphore_signal(
            hello, inc=1, device_id=(member(line, place), tile), device_id_type=MESH
        )
        return carry

    lax.fori_loop(skip_line, x, hello_line, 0)

    def halo_copy(side, s, far):
        where = my_part if far else pl.ds(0, cols)
        return pltpu.make_async_remote_copy(
            src_ref=own.at[s, edge_rows[side], where], dst_ref=halo.at[side, s, :, where],
            send_sem=halo_send.at[side, s], recv_sem=halo_recv.at[side, s],
            device_id=up if side == 0 else down, device_id_type=MESH,
        )

    def share_copy(side, s, step):
        return pltpu.make_async_remote_copy(
            src_ref=halo.at[side, s, :, my_part], dst_ref=halo.at[side, s, :, my_part],
            send_sem=share_send, recv_sem=share_recv.at[side, s, step - 1],
            device_id=(line_peer(step), tile), device_id_type=MESH,
        )

    def share_arrival(side, s, step):
        theirs = lax.rem(x + lines - step, lines)
        where = pl.ds(pl.multiple_of(theirs * part, part), part)
        return pltpu.make_async_remote_copy(
            src_ref=halo.at[side, s, :, where], dst_ref=halo.at[side, s, :, where],
            send_sem=share_send, recv_sem=share_recv.at[side, s, step - 1],
            device_id=(member(theirs, place), tile), device_id_type=MESH,
        )

    for copy in own_copies:
        copy.wait()
    for s in range(slices):
        for side, far in ((0, across_up), (1, across_down)):

            @pl.when(jnp.logical_and(late, far))
            def _():
                halo_copy(side, s, True).start()

            @pl.when(jnp.logical_not(far))
            def _():
                halo_copy(side, s, False).start()

    small_copies[2].wait()
    small_copies[3].wait()
    u, half = beam // 2, lax.rem(beam, 2)
    tiles = cols // 128
    extent = strip + 2 * HALO
    matrix0[...] = blur_matrix(0)
    matrix1[...] = blur_matrix(REACH)
    spread[0], spread[1] = spread_matrix()
    place_rows(ext, own, HALO, extent)

    @pl.when(jnp.logical_and(x < lines - 1, jnp.logical_not(first_one)))
    def _():
        pl.semaphore_wait(hello, lines - 1 - x)

    @pl.when(jnp.logical_and(early, jnp.logical_not(first_one)))
    def _():
        lax.fori_loop(x + 1, lines, send_line, 0)

    def collect(z, carry):
        for line in range(lines):
            row_arrival(line, z).wait_recv()
        return carry

    windows = ((first, 1, 32, matrix0, trans0), (second, 6, 24, matrix1, trans1))

    def near_windows():
        for s, (gathered, row, count, _, _) in enumerate(windows):
            for side, far in ((0, across_down), (1, across_up)):

                @pl.when(jnp.logical_not(far))
                def _():
                    halo_copy(side, s, False).wait_recv()
                    place_halo(ext, halo, side, s, extent, strip)

            take_windows(
                ext, extent, tiles, probe_rows, probe_cols, gathered, s, row, count, u, half
            )

    @pl.when(across)
    def _():
        for s in range(slices):
            for side, far in ((0, across_down), (1, across_up)):

                @pl.when(far)
                def _():
                    clear_halo(ext, side, s, tiles, extent, strip)

        near_windows()

    def answer(z, carry):
        for line in range(lines):
            row_arrival(line, z).wait_recv()
            row_copy(line, z).start()
        return carry

    for side, far in ((0, across_up), (1, across_down)):

        @pl.when(jnp.logical_and(early, far))
        def _():
            pl.semaphore_wait(ready_edge, 1)
            for s in range(slices):
                halo_copy(side, s, True).start()

    answer_first = jnp.logical_or(across, place >= group // 2)

    @pl.when(jnp.logical_and(jnp.logical_and(early, answer_first), jnp.logical_not(first_one)))
    def _():
        lax.fori_loop(place + 1, group, answer, 0)

    def collect_rows():
        @pl.when(jnp.logical_not(answer_first))
        def _():
            lax.fori_loop(place + 1, group, answer, 0)

        @pl.when(jnp.logical_and(on_first, place > 0))
        def _():
            row_arrival(0, 0).wait_recv()

        def collect_line(line, carry):
            row_arrival(line, place).wait_recv()
            return carry

        def collect_head(line, carry):
            row_arrival(line, 0).wait_recv()
            return carry

        lax.fori_loop(skip_line, x, collect_line, 0)

        @pl.when(jnp.logical_not(first_one))
        def _():
            lax.fori_loop(x + 1, lines, collect_line, 0)

        @pl.when(place > 0)
        def _():
            lax.fori_loop(skip_first, lines, collect_head, 0)

        lax.fori_loop(1, place, collect, 0)

        @pl.when(first_one)
        def _():
            first_copy.wait_recv()

        @pl.when(feeder)
        def _():
            first_copy.start()

        pl.semaphore_wait(ready, 1)

        @pl.when(first_one)
        def _():
            first_table_copy.start()

        @pl.when(jnp.logical_not(first_one))
        def _():
            table_copy.start()


    beside_first = jnp.logical_and(skip_line == 1, beam > 0)

    @pl.when(beside_first)
    def _():
        row_arrival(0, 0).wait_recv()

    for s in range(slices):
        for side, far in ((0, across_down), (1, across_up)):

            @pl.when(far)
            def _():
                halo_copy(side, s, True).wait_recv()
                for step in range(1, lines):
                    share_copy(side, s, step).start()


    @pl.when(jnp.logical_and(jnp.logical_and(early, across), jnp.logical_not(first_one)))
    def _():
        collect_rows()

    for s, (gathered, row, _, matrix, trans) in enumerate(windows):
        if s == 0:
            @pl.when(jnp.logical_not(across))
            def _():
                near_windows()

        for side, far in ((0, across_down), (1, across_up)):

            @pl.when(far)
            def _():
                for step in range(1, lines):
                    share_arrival(side, s, step).wait_recv()
                place_halo(ext, halo, side, s, extent, strip)
                take_windows(
                    ext, extent, tiles, probe_rows, probe_cols, gathered, s, row, 16, u, half,
                    base=0 if side == 0 else gathered.shape[0] // 32 - 16,
                )

        transmission(gathered, blurred, matrix, trans)

    @pl.when(jnp.logical_or(first_one, jnp.logical_and(early, jnp.logical_not(across))))
    def _():
        collect_rows()

    @pl.when(late)
    def _():
        table_copy.wait_recv()

    rows = jnp.where(first_one, whole[:, 0, :], table[:, 0, :])
    wave[...] = probe_function(rows, u, half)
    result = propagate(wave, trans0, trans1, psi, both, spread, table.shape[0])
    turned = jnp.transpose(result)
    out[:, 0:32] = turned[0:8]
    out[:, 32:64] = turned[64:72]

    def sent(ref, semaphore):
        pltpu.make_async_remote_copy(
            src_ref=ref, dst_ref=ref, send_sem=semaphore, recv_sem=table_recv,
            device_id=other_half, device_id_type=MESH,
        ).wait_send()

    for s in range(slices):
        for side, far in ((0, across_up), (1, across_down)):

            @pl.when(far)
            def _():
                halo_copy(side, s, True).wait_send()

            @pl.when(jnp.logical_not(far))
            def _():
                halo_copy(side, s, False).wait_send()

    @pl.when(across)
    def _():
        sent(halo.at[0, :, :, pl.ds(0, (lines - 1) * part)], share_send)


    @pl.when(early)
    def _():
        table_copy.wait_send()


        @pl.when(jnp.logical_and(on_first, beam > 0))
        def _():
            sent(table.at[pl.ds(0, lines * group - 2)], row_send)

        @pl.when(jnp.logical_not(jnp.logical_and(on_first, beam > 0)))
        def _():
            sent(table.at[pl.ds(0, lines * group - 1)], row_send)

    @pl.when(feeder)
    def _():
        first_copy.wait_send()


def body(atom_counts, beam_index, beam_weight, probe_rows, probe_cols):
    slices, strip, cols = atom_counts.shape
    beams = lax.axis_size("beam")
    lines = beams // 8
    hbm = pl.BlockSpec(memory_space=pltpu.HBM)
    dma = pltpu.SemaphoreType.DMA
    result = pl.pallas_call(
        kernel,
        out_shape=pltpu.VMEM((8, probe_rows.shape[0]), F32),
        in_specs=[hbm] * 5,
        out_specs=pl.BlockSpec(memory_space=pltpu.VMEM),
        scratch_shapes=[
            pltpu.SMEM(probe_rows.shape, jnp.int32),
            pltpu.SMEM(probe_cols.shape, jnp.int32),
            pltpu.SMEM(beam_index.shape, jnp.int32),
            pltpu.SMEM(beam_weight.shape, F32),
            pltpu.VMEM((slices, strip, cols), BF16),
            pltpu.VMEM((2, slices, HALO, cols), BF16),
            pltpu.VMEM((beams, 1, 128), F32),
            pltpu.VMEM((beams, 1, 128), F32),
            pltpu.VMEM((slices * (strip + 2 * HALO) * cols // 128, 128), F32),
            pltpu.VMEM((32 * 32, 128), F32),
            pltpu.VMEM((24 * 32, 128), F32),
            pltpu.VMEM((32 * 32, 128), F32),
            pltpu.VMEM((128, 256), BF16),
            pltpu.VMEM((128, 256), BF16),
            pltpu.VMEM((2, 256, 256), BF16),
            pltpu.VMEM((2, 21 * 32, 128), F32),
            pltpu.VMEM((2, 11 * 32, 128), F32),
            pltpu.VMEM((128, 256), F32),
            pltpu.VMEM((2, 21 * 32, 128), F32),
            pltpu.VMEM((11 * 32, 256), F32),
            dma((2, slices)),
            dma((4,)),
            dma((2, slices)),
            dma((2, slices)),
            dma(()),
            dma((2, slices, lines - 1)),
            dma(()),
            dma((beams,)),
            dma(()),
            dma(()),
            dma(()),
            dma(()),
            pltpu.SemaphoreType.REGULAR,
            pltpu.SemaphoreType.REGULAR,
            pltpu.SemaphoreType.REGULAR,
        ],
        compiler_params=pltpu.CompilerParams(
            collective_id=0, has_side_effects=True, vmem_limit_bytes=64 * 2**20 - 2**18
        ),
    )(probe_rows, probe_cols, beam_index, beam_weight, atom_counts)
    return result.T


def solution(mesh):
    return jax.shard_map(
        body,
        mesh=mesh,
        in_specs=(P(None, "tile", None), P("beam", None), P("beam"), P("tile"), P("tile")),
        out_specs=P("tile", "beam"),
        check_vma=False,
    )
```
